32 devices in a mesh: replica: 2 (over core), fsdp: 4 (over y, x), tensor: 4 (over z).
Axes of the slice: x: 2, y: 2, z: 4, core: 2. Of those that a mesh axis runs over, the one named last changes fastest.
Arguments:
- grads: bfloat16 [2, 2, 4096, 14336], P('replica', None, 'fsdp', 'tensor'), may hold values from -6 to 6
- momentum: bfloat16 [2, 4096, 14336], P(None, 'fsdp', 'tensor'), may hold values from -50 to 50, as said below
- basis: bfloat16 [2, 14336, 512], P(None, 'tensor'), may hold values from -0.046875 to 0.046875
Outputs:
- momentum_new: bfloat16 [2, 4096, 14336], P(None, 'fsdp', 'tensor')
- update: bfloat16 [2, 4096, 14336], P(None, 'fsdp', 'tensor')
- basis_new: bfloat16 [2, 14336, 512], P(None, 'tensor')
The draws below stay inside these ranges and needn't reach their ends.
Inputs may be any that keep to these rules, and one draw needn't show every extreme that they name: `momentum`: entries are finite.
All inputs are finite; a program needn't handle non-finite values.
Results may differ from the reference program's by a relative error of at most 0.028.
Values may be sent and summed in bfloat16 or wider, within the bound.
No kernel may reach another device: no remote copies, remote signals or barrier semaphores. Data moves between devices by JAX's collectives and lax.ppermute only.
A program may use at most 192 MiB of HBM per device.

```python
import math
import jax
import jax.numpy as jnp
from jax import lax

FEATURES = 4096
UNITS = 14336
RANK = 512
WEIGHTS = 2
REPLICAS = 2


def draw_momentum(key, part):
    first, second, third = jax.random.split(key, 3)
    shape = (WEIGHTS, FEATURES, UNITS)
    base = jnp.clip(jax.random.normal(first, shape, jnp.float32), -5.0, 5.0)
    top = math.log(10.0)
    row_scale = jnp.exp(jax.random.uniform(second, (WEIGHTS, FEATURES, 1), jnp.float32, 0.0, top) - 0.5 * top)
    col_scale = jnp.exp(jax.random.uniform(third, (WEIGHTS, 1, UNITS), jnp.float32, 0.0, top) - 0.5 * top)
    return (base * row_scale * col_scale).astype(jnp.bfloat16)


def levels(own_key, shape, cuts, least, top_value):
    gain, own = 1.0, jax.random.fold_in(own_key, 6)
    for position, parts in cuts:
        steps = jnp.exp(jax.random.uniform(jax.random.fold_in(own, position), (parts,), jnp.float32, least / len(cuts), top_value / len(cuts)))
        gain = gain * jnp.repeat(steps, shape[position] // parts).reshape([-1 if axis == position else 1 for axis in range(len(shape))])
    return gain


def scatter_about(key, dims, scale, limit, cuts=(), held_as=jnp.bfloat16):
    factor_of = levels(key, dims, cuts, -0.22, 0.18) if cuts else 1.0
    drawn = jax.random.normal(key, dims, jnp.float32) * scale * factor_of
    return jnp.minimum(jnp.maximum(drawn, -limit), limit).astype(held_as)


def setup_inputs(seed: int = 0) -> dict:
    key_list = jax.random.split(jax.random.key(seed), 4)
    return {
        "grads": scatter_about(key_list[0], (REPLICAS, WEIGHTS, FEATURES, UNITS), 1.0, 6.0, ((0, 2), (2, 4), (3, 4))),
        "momentum": draw_momentum(jax.random.fold_in(key_list[3], 71), 0),
        "basis": scatter_about(key_list[2], (WEIGHTS, UNITS, RANK), UNITS ** -0.5, 0.046875, ((1, 4),)),
    }


momentum_decay = 0.95

def one_weight(grad_stack, moment, right):
    total_grad = lax.optimization_barrier(jnp.sum(grad_stack.astype(jnp.float32), axis=0))
    blended = (moment.astype(jnp.float32) + total_grad).astype(jnp.bfloat16)
    projected = jnp.dot(blended.astype(jnp.float32), right.astype(jnp.float32), preferred_element_type=jnp.float32)
    gram_matrix = jnp.dot(projected.T.astype(jnp.float32), projected.astype(jnp.float32), preferred_element_type=jnp.float32, precision=lax.Precision.HIGHEST)
    factor = jnp.linalg.cholesky(gram_matrix)
    left_basis = jax.scipy.linalg.solve_triangular(factor, projected.T, lower=True).T.astype(jnp.bfloat16)
    back = jnp.dot(blended.T.astype(jnp.float32), left_basis.astype(jnp.float32), preferred_element_type=jnp.float32)
    col_norm = jnp.sqrt(lax.optimization_barrier(jnp.sum(back * back, axis=0))) + 1e-06
    back_b = back.astype(jnp.bfloat16)
    basis_new = (back_b.astype(jnp.float32) / col_norm[None, :]).astype(jnp.bfloat16)
    feedback = jnp.dot(left_basis.astype(jnp.float32), back_b.T.astype(jnp.float32), preferred_element_type=jnp.float32)
    momentum_new = (blended.astype(jnp.float32) - (1.0 - momentum_decay) * feedback).astype(jnp.bfloat16)
    scale = math.sqrt(FEATURES * UNITS / RANK)
    update = (scale * jnp.dot(left_basis.astype(jnp.float32), basis_new.T.astype(jnp.float32), preferred_element_type=jnp.float32)).astype(jnp.bfloat16)
    return (momentum_new, update, basis_new)

def reference(grads, momentum, basis):
    moments, updates, bases = ([], [], [])
    for which in range(WEIGHTS):
        result = one_weight(grads[:, which], momentum[which], basis[which])
        moments.append(result[0])
        updates.append(result[1])
        bases.append(result[2])
    return (jnp.stack(moments), jnp.stack(updates), jnp.stack(bases))
```

```python
import functools
import math

import jax
import jax.numpy as jnp
from jax import lax
from jax.experimental import pallas as pl
from jax.experimental.pallas import tpu as pltpu
from jax.sharding import PartitionSpec as P

LANES = 128
SUBS = 8
TILE = 512
momentum_decay = 0.95


def invert_block(rows):
    count = len(rows)
    lane = lax.broadcasted_iota(jnp.int32, (SUBS, LANES), 1)
    sub = lax.broadcasted_iota(jnp.int32, (SUBS, LANES), 0)
    rows = list(rows)
    wide = lambda v, i: jnp.broadcast_to(v[i:i+1, :], (SUBS, LANES))
    col = lambda v, c: jnp.broadcast_to(v[:, c:c+1], (SUBS, LANES))
    for p in range(count):
        base = p * SUBS
        inside = (lane >= base) & (lane < base + SUBS)
        mine = rows[p]
        cols = [col(mine, base + i) for i in range(SUBS)]
        solved = jnp.where(inside, jnp.where(lane == base + sub, 1.0, 0.0), mine)
        half = solved
        for i in range(SUBS):
            pivot = wide(cols[i], i)
            inverse = 1.0 / pivot
            at = sub == i
            gain = jnp.where(at, 1.0 - inverse, cols[i] * inverse)
            for j in range(i + 1, SUBS):
                cols[j] = cols[j] - gain * wide(cols[j], i)
            row = wide(solved, i)
            half = jnp.where(at, row * lax.rsqrt(pivot), half)
            solved = solved - gain * row
        rows[p] = jnp.where(lane < base + SUBS, half, 0.0)
        if p + 1 < count:
            wides = [wide(solved, i) for i in range(SUBS)]
            for q in range(p + 1, count):
                below = rows[q]
                terms = [col(below, base + i) * wides[i] for i in range(SUBS)]
                while len(terms) > 1:
                    terms = [a + b for a, b in zip(terms[::2], terms[1::2])]
                rows[q] = jnp.where(inside, 0.0, below) - terms[0]
    return rows


def chol_kernel(gram_ref, hi_ref, lo_ref, work, part):
    blocks = gram_ref.shape[0] // LANES
    for c in range(blocks):
        work[c] = gram_ref[:, c * LANES:(c + 1) * LANES]
    dot = functools.partial(lax.dot_general, preferred_element_type=jnp.float32, precision=lax.Precision.HIGHEST)

    def step(k, carry):
        start = pl.multiple_of(k * LANES, LANES)
        rows = [work[k, pl.ds(start + SUBS * q, SUBS), :] for q in range(LANES // SUBS)]
        inv = jnp.concatenate(invert_block(rows), axis=0)
        for c in range(blocks):
            part[c] = dot(inv, work[c, pl.ds(start, LANES), :], (((1,), (0,)), ((), ())))
        part[k] = inv
        for c in range(blocks):
            work[c, pl.ds(start, LANES), :] = part[c]
        for r in range(1, blocks):
            @pl.when(r > k)
            def _():
                work[k, r * LANES:(r + 1) * LANES, :] = jnp.zeros((LANES, LANES), jnp.float32)
                left = part[r]
                for c in range(blocks):
                    work[c, r * LANES:(r + 1) * LANES, :] -= dot(left, part[c], (((0,), (0,)), ((), ())))
        return carry

    lax.fori_loop(0, blocks, step, 0)
    row = lax.broadcasted_iota(jnp.int32, gram_ref.shape, 0)
    lane = lax.broadcasted_iota(jnp.int32, gram_ref.shape, 1)
    for c in range(blocks):
        cut = slice(c * LANES, (c + 1) * LANES)
        value = jnp.where(row[:, cut] >= lane[:, cut], work[c], 0.0)
        high = value.astype(jnp.bfloat16)
        hi_ref[:, cut] = high
        lo_ref[:, cut] = (value - high.astype(jnp.float32)).astype(jnp.bfloat16)


def inverse_factor(gram):
    n = gram.shape[0]
    return pl.pallas_call(
        chol_kernel,
        out_shape=[jax.ShapeDtypeStruct((n, n), jnp.bfloat16)] * 2,
        in_specs=[pl.BlockSpec(memory_space=pltpu.VMEM)],
        out_specs=[pl.BlockSpec(memory_space=pltpu.VMEM)] * 2,
        scratch_shapes=[pltpu.VMEM((n // LANES, n, LANES), jnp.float32), pltpu.VMEM((n // LANES, LANES, LANES), jnp.float32)],
        compiler_params=pltpu.CompilerParams(vmem_limit_bytes=32 << 20),
        name="inverse_factor",
    )(gram)


def tile_of(size):
    return TILE if size % TILE == 0 else size


def partial_kernel(which_ref, grads_ref, *refs, with_moment):
    if with_moment:
        moment_ref, basis_ref, out_ref, total = refs
        rows = (grads_ref[...].astype(jnp.float32) + moment_ref[...].astype(jnp.float32)).astype(jnp.bfloat16)
    else:
        basis_ref, out_ref, total = refs
        rows = grads_ref[...]
    step = pl.program_id(0)
    product = jnp.dot(rows, basis_ref[...], preferred_element_type=jnp.float32)

    @pl.when(step == 0)
    def _():
        total[...] = product

    @pl.when(step > 0)
    def _():
        total[...] += product

    @pl.when(step == pl.num_programs(0) - 1)
    def _():
        out_ref[...] = total[...].astype(out_ref.dtype)


def partial_projection(which, grads, moment, basis):
    _, rows, units = grads.shape
    rank = basis.shape[-1]
    tile = tile_of(units)
    columns = pl.BlockSpec((None, rows, tile), lambda step, which_ref: (which_ref[0], 0, step))
    factors = pl.BlockSpec((None, tile, rank), lambda step, which_ref: (which_ref[0], step, 0))
    wide = [grads] if moment is None else [grads, moment]
    return pl.pallas_call(
        functools.partial(partial_kernel, with_moment=moment is not None),
        grid_spec=pltpu.PrefetchScalarGridSpec(
            num_scalar_prefetch=1,
            grid=(units // tile,),
            in_specs=[columns] * len(wide) + [factors],
            out_specs=pl.BlockSpec((rows, rank), lambda step, which_ref: (0, 0)),
            scratch_shapes=[pltpu.VMEM((rows, rank), jnp.float32)],
        ),
        out_shape=jax.ShapeDtypeStruct((rows, rank), jnp.bfloat16),
        compiler_params=pltpu.CompilerParams(vmem_limit_bytes=48 << 20),
        name="partial_projection",
    )(which, *wide, basis)


def output_kernel(which_ref, left_ref, back_ref, inverse_ref, blended_ref, *refs, scale):
    momentum_ref, update_ref, basis_ref = refs[-3:]
    dims = (((1,), (1,)), ((), ()))
    left = left_ref[...]
    back = back_ref[...]
    feedback = lax.dot_general(left, back, dims, preferred_element_type=jnp.float32)
    momentum_ref[...] = (blended_ref[...].astype(jnp.float32) - (1.0 - momentum_decay) * feedback).astype(jnp.bfloat16)
    normed = (back.astype(jnp.float32) * inverse_ref[...]).astype(jnp.bfloat16)
    basis_ref[...] = normed
    update_ref[...] = (scale * lax.dot_general(left, normed, dims, preferred_element_type=jnp.float32)).astype(jnp.bfloat16)


def write_outputs(which, left, back, inverse, blended, earlier, scale):
    rows, units = blended.shape
    rank = left.shape[1]
    tile = tile_of(units)
    columns = pl.BlockSpec((None, rows, tile), lambda step, which_ref: (which_ref[0], 0, step))
    return pl.pallas_call(
        functools.partial(output_kernel, scale=scale),
        grid_spec=pltpu.PrefetchScalarGridSpec(
            num_scalar_prefetch=1,
            grid=(units // tile,),
            in_specs=[
                pl.BlockSpec((rows, rank), lambda step, which_ref: (0, 0)),
                pl.BlockSpec((tile, rank), lambda step, which_ref: (step, 0)),
                pl.BlockSpec((1, rank), lambda step, which_ref: (0, 0)),
                pl.BlockSpec((rows, tile), lambda step, which_ref: (0, step)),
            ]
            + [pl.BlockSpec(memory_space=pl.ANY)] * len(earlier),
            out_specs=[
                columns,
                columns,
                pl.BlockSpec((None, tile, rank), lambda step, which_ref: (which_ref[0], step, 0)),
            ],
        ),
        out_shape=[
            jax.ShapeDtypeStruct((2, rows, units), jnp.bfloat16),
            jax.ShapeDtypeStruct((2, rows, units), jnp.bfloat16),
            jax.ShapeDtypeStruct((2, units, rank), jnp.bfloat16),
        ],
        input_output_aliases={5 + i: i for i in range(len(earlier))},
        compiler_params=pltpu.CompilerParams(vmem_limit_bytes=48 << 20),
        name="write_outputs",
    )(which, left, back, inverse, blended, *earlier)


def swap(value, axis, bit, size):
    return lax.ppermute(value, axis, [(i, i ^ bit) for i in range(size)])


def bits_of(size):
    return [1 << i for i in range(size.bit_length() - 1)]


def added(first, second):
    return (first.astype(jnp.float32) + second.astype(jnp.float32)).astype(first.dtype)


def halved(value, axis, bit):
    high = (lax.axis_index(axis) & bit) != 0
    size = value.shape[0] // 2
    first, second = value[:size], value[size:]
    return jnp.where(high, second, first), jnp.where(high, first, second)


def joined(mine, theirs, axis, bit):
    high = (lax.axis_index(axis) & bit) != 0
    return jnp.where(high, jnp.concatenate([theirs, mine]), jnp.concatenate([mine, theirs]))


def reduce_all(values, axis, size, orders):
    values = list(values)
    steps = len(orders[0])
    for step in range(steps):
        for i, order in enumerate(orders):
            keep, send = halved(values[i], axis, order[step])
            values[i] = added(keep, swap(send, axis, order[step], size))
    for step in reversed(range(steps)):
        for i, order in enumerate(orders):
            values[i] = joined(values[i], swap(values[i], axis, order[step], size), axis, order[step])
    return values


def double_all(values, axis, size, orders):
    values = list(values)
    for step in range(len(orders[0])):
        for i, order in enumerate(orders):
            values[i] = added(values[i], swap(values[i], axis, order[step], size))
    return values


def times_inverse(rows, high, low):
    dims = (((1,), (1,)), ((), ()))
    return lax.dot_general(rows, high, dims, preferred_element_type=jnp.float32) + lax.dot_general(
        rows, low, dims, preferred_element_type=jnp.float32
    )


def shards(grads, momentum, basis, *, sizes):
    owner = lax.axis_index("replica")
    own = owner.astype(jnp.int32).reshape(1)
    other = 1 - own
    grads = grads[0]
    fsdp, tensor = sizes["fsdp"], sizes["tensor"]
    bits = bits_of(fsdp)
    orders = [bits, bits[::-1]]

    sent = partial_projection(other, grads, None, basis)
    received = swap(sent, "replica", 1, 2)
    mine = partial_projection(own, grads, momentum, basis)
    (projected,) = reduce_all([added(mine, received)], "tensor", tensor, [bits_of(tensor)])

    theirs = swap(lax.dynamic_index_in_dim(grads, other[0], 0, keepdims=False), "replica", 1, 2)
    total = lax.dynamic_index_in_dim(grads, owner, 0, keepdims=False).astype(jnp.float32) + theirs.astype(jnp.float32)
    blended = (lax.dynamic_index_in_dim(momentum, owner, 0, keepdims=False).astype(jnp.float32) + total).astype(
        jnp.bfloat16
    )
    blended_other = swap(blended, "replica", 1, 2)

    gram = lax.dot_general(
        projected, projected, (((0,), (0,)), ((), ())), preferred_element_type=jnp.float32
    ).astype(jnp.bfloat16)
    half = gram.shape[0] // 2
    gram = jnp.concatenate(double_all([gram[:half], gram[half:]], "fsdp", fsdp, orders))
    high, low = inverse_factor(gram.astype(jnp.float32))

    crossed = lax.dot_general(
        blended, projected, (((0,), (0,)), ((), ())), preferred_element_type=jnp.float32
    ).astype(jnp.bfloat16)
    half = crossed.shape[0] // 2
    crossed = jnp.concatenate(reduce_all([crossed[:half], crossed[half:]], "fsdp", fsdp, orders))

    left = times_inverse(projected, high, low).astype(jnp.bfloat16)
    back = times_inverse(crossed, high, low)
    squares = jnp.sum(back * back, axis=0, keepdims=True)
    (squares,) = double_all([squares], "tensor", tensor, [bits_of(tensor)])
    back = back.astype(jnp.bfloat16)
    inverse = 1.0 / (jnp.sqrt(squares) + 1e-06)
    left_other = swap(left, "replica", 1, 2)
    back_other = swap(back, "replica", 1, 2)
    inverse_other = swap(inverse, "replica", 1, 2)

    scale = math.sqrt(grads.shape[1] * fsdp * grads.shape[2] * tensor / basis.shape[-1])
    outputs = write_outputs(own, left, back, inverse, blended, (), scale)
    return tuple(write_outputs(other, left_other, back_other, inverse_other, blended_other, outputs, scale))


def solution(mesh):
    placed = (
        P("replica", None, "fsdp", "tensor"),
        P(None, "fsdp", "tensor"),
        P(None, "tensor", None),
    )
    return jax.shard_map(
        functools.partial(shards, sizes=dict(mesh.shape)),
        mesh=mesh,
        in_specs=placed,
        out_specs=(P(None, "fsdp", "tensor"), P(None, "fsdp", "tensor"), P(None, "tensor", None)),
        check_vma=False,
    )
```

```python
import functools
import math

import jax
import jax.numpy as jnp
from jax import lax
from jax.experimental import pallas as pl
from jax.experimental.pallas import tpu as pltpu
from jax.sharding import PartitionSpec as P

LANES = 128
SUBS = 8
TILE = 896
BLOCKS = 4
momentum_decay = 0.95


def invert_block(rows):
    count = len(rows)
    lane = lax.broadcasted_iota(jnp.int32, (SUBS, LANES), 1)
    sub = lax.broadcasted_iota(jnp.int32, (SUBS, LANES), 0)
    rows = list(rows)
    wide = lambda v, i: jnp.broadcast_to(v[i:i+1, :], (SUBS, LANES))
    col = lambda v, c: jnp.broadcast_to(v[:, c:c+1], (SUBS, LANES))
    for p in range(count):
        base = p * SUBS
        inside = (lane >= base) & (lane < base + SUBS)
        mine = rows[p]
        cols = [col(mine, base + i) for i in range(SUBS)]
        solved = jnp.where(inside, jnp.where(lane == base + sub, 1.0, 0.0), mine)
        half = solved
        for i in range(SUBS):
            pivot = wide(cols[i], i)
            inverse = 1.0 / pivot
            at = sub == i
            gain = jnp.where(at, 1.0 - inverse, cols[i] * inverse)
            for j in range(i + 1, SUBS):
                cols[j] = cols[j] - gain * wide(cols[j], i)
            row = wide(solved, i)
            half = jnp.where(at, row * lax.rsqrt(pivot), half)
            solved = solved - gain * row
        rows[p] = jnp.where(lane < base + SUBS, half, 0.0)
        if p + 1 < count:
            wides = [wide(solved, i) for i in range(SUBS)]
            for q in range(p + 1, count):
                below = rows[q]
                terms = [col(below, base + i) * wides[i] for i in range(SUBS)]
                while len(terms) > 1:
                    terms = [a + b for a, b in zip(terms[::2], terms[1::2])]
                rows[q] = jnp.where(inside, 0.0, below) - terms[0]
    return rows


def chol_kernel(*refs, k, blocks):
    last = k == blocks - 1
    source, part = refs[0], refs[-1]
    work = refs[1]
    if k == 0:
        for c in range(blocks):
            work[c] = source[:, c * LANES : (c + 1) * LANES].astype(jnp.float32)
        held = work
    else:
        held = source
    dot = functools.partial(lax.dot_general, preferred_element_type=jnp.float32, precision=lax.Precision.HIGHEST)
    start = k * LANES
    mine = slice(start, start + LANES)
    inv = jnp.concatenate(
        invert_block([held[k, start + SUBS * q : start + SUBS * (q + 1), :] for q in range(LANES // SUBS)]), axis=0
    )
    for c in range(blocks):
        part[c] = inv if c == k else dot(inv, held[c, mine, :], (((1,), (0,)), ((), ())))
    if not last:
        for c in range(blocks):
            if k > 0:
                work[c, :start, :] = held[c, :start, :]
            work[c, mine, :] = part[c]
        for r in range(k + 1, blocks):
            rows = slice(r * LANES, (r + 1) * LANES)
            for c in range(blocks):
                if c > k and c < r:
                    continue
                product = dot(part[r], part[c], (((0,), (0,)), ((), ())))
                work[c, rows, :] = -product if c == k else held[c, rows, :] - product
        return
    high_ref, low_ref = refs[1:3]
    for r in range(blocks):
        rows = slice(r * LANES, (r + 1) * LANES)
        for c in range(blocks):
            cut = slice(c * LANES, (c + 1) * LANES)
            if c > r:
                high_ref[rows, cut] = jnp.zeros((LANES, LANES), jnp.bfloat16)
                low_ref[rows, cut] = jnp.zeros((LANES, LANES), jnp.bfloat16)
                continue
            value = part[c] if r == k else held[c, rows, :]
            high = value.astype(jnp.bfloat16)
            high_ref[rows, cut] = high
            low_ref[rows, cut] = (value - high.astype(jnp.float32)).astype(jnp.bfloat16)


def chol_step(value, k, size):
    blocks = size // LANES
    if k == blocks - 1:
        out_shape = [jax.ShapeDtypeStruct((size, size), jnp.bfloat16)] * 2
    else:
        out_shape = [jax.ShapeDtypeStruct((blocks, size, LANES), jnp.float32)]
    results = pl.pallas_call(
        functools.partial(chol_kernel, k=k, blocks=blocks),
        out_shape=out_shape,
        in_specs=[pl.BlockSpec(memory_space=pltpu.VMEM)],
        out_specs=[pl.BlockSpec(memory_space=pltpu.VMEM)] * len(out_shape),
        scratch_shapes=[pltpu.VMEM((blocks, LANES, LANES), jnp.float32)],
        compiler_params=pltpu.CompilerParams(vmem_limit_bytes=16 << 20),
        name="chol_step",
    )(value)
    return results if k == blocks - 1 else results[0]


def tile_of(size):
    return TILE if size % TILE == 0 else size


def partial_kernel(which_ref, grads_ref, moment_ref, basis_ref, sent_ref, mine_ref, total):
    weight, step = pl.program_id(0), pl.program_id(1)
    last = step == pl.num_programs(1) - 1

    def add(product):
        @pl.when(step == 0)
        def _():
            total[...] = product

        @pl.when(step > 0)
        def _():
            total[...] += product

    @pl.when(weight == 0)
    def _():
        add(jnp.dot(grads_ref[...], basis_ref[...], preferred_element_type=jnp.float32))

        @pl.when(last)
        def _():
            sent_ref[...] = total[...].astype(sent_ref.dtype)

    @pl.when(weight == 1)
    def _():
        rows = (grads_ref[...].astype(jnp.float32) + moment_ref[...].astype(jnp.float32)).astype(jnp.bfloat16)
        add(jnp.dot(rows, basis_ref[...], preferred_element_type=jnp.float32))

        @pl.when(last)
        def _():
            mine_ref[...] = total[...].astype(mine_ref.dtype)


def partial_projection(own, grads, moment, basis):
    _, rows, units = grads.shape
    rank = basis.shape[-1]
    tile = tile_of(units)

    def weight_of(weight, own_ref):
        return jnp.where(weight == 0, 1 - own_ref[0], own_ref[0])

    whole = pl.BlockSpec((rows, rank), lambda weight, step, own_ref: (0, 0))
    return pl.pallas_call(
        partial_kernel,
        grid_spec=pltpu.PrefetchScalarGridSpec(
            num_scalar_prefetch=1,
            grid=(2, units // tile),
            in_specs=[
                pl.BlockSpec((None, rows, tile), lambda weight, step, own_ref: (weight_of(weight, own_ref), 0, step)),
                pl.BlockSpec((None, rows, tile), lambda weight, step, own_ref: (own_ref[0], 0, step * weight)),
                pl.BlockSpec((None, tile, rank), lambda weight, step, own_ref: (weight_of(weight, own_ref), step, 0)),
            ],
            out_specs=[whole, whole],
            scratch_shapes=[pltpu.VMEM((rows, rank), jnp.float32)],
        ),
        out_shape=[jax.ShapeDtypeStruct((rows, rank), jnp.bfloat16)] * 2,
        compiler_params=pltpu.CompilerParams(vmem_limit_bytes=48 << 20),
        name="partial_projection",
    )(own, grads, moment, basis)


ROWS_BY_ROWS = (((1,), (1,)), ((), ()))
COLUMNS_BY_COLUMNS = (((0,), (0,)), ((), ()))
ROOMY = 48 << 20


def fixed(shape):
    return pl.BlockSpec(shape, lambda step, *_: (0,) * len(shape))


def cross_kernel(ids_ref, blended_ref, projected_ref, first_ref, second_ref):
    product = lax.dot_general(
        blended_ref[...], projected_ref[...], COLUMNS_BY_COLUMNS, preferred_element_type=jnp.float32
    ).astype(jnp.bfloat16)
    for step, ref in enumerate((first_ref, second_ref)):

        @pl.when(pl.program_id(0) == step)
        def _():
            ref[...] = product


def cross(ids, blended, projected):
    rows, rank = projected.shape
    block = blended.shape[1] // BLOCKS
    return pl.pallas_call(
        cross_kernel,
        grid_spec=pltpu.PrefetchScalarGridSpec(
            num_scalar_prefetch=1,
            grid=(2,),
            in_specs=[pl.BlockSpec((rows, block), lambda step, ids_ref: (0, ids_ref[step])), fixed((rows, rank))],
            out_specs=[fixed((block, rank))] * 2,
        ),
        out_shape=[jax.ShapeDtypeStruct((block, rank), jnp.bfloat16)] * 2,
        compiler_params=pltpu.CompilerParams(vmem_limit_bytes=ROOMY),
        name="cross",
    )(ids, blended, projected)


def back_kernel(first_ref, second_ref, high_ref, low_ref, back_ref, squares_ref):
    step = pl.program_id(0)

    def run(ref):
        rows = ref[...]
        back = lax.dot_general(rows, high_ref[...], ROWS_BY_ROWS, preferred_element_type=jnp.float32)
        back += lax.dot_general(rows, low_ref[...], ROWS_BY_ROWS, preferred_element_type=jnp.float32)
        back_ref[...] = back.astype(jnp.bfloat16)
        return jnp.sum(back * back, axis=0, keepdims=True)

    @pl.when(step == 0)
    def _():
        squares_ref[...] = run(first_ref)

    @pl.when(step == 1)
    def _():
        squares_ref[...] += run(second_ref)


def times_inverse(first, second, high, low):
    block, rank = first.shape
    return pl.pallas_call(
        back_kernel,
        grid=(2,),
        in_specs=[fixed((block, rank))] * 2 + [fixed((rank, rank))] * 2,
        out_specs=[pl.BlockSpec((block, rank), lambda step: (step, 0)), fixed((1, rank))],
        out_shape=[jax.ShapeDtypeStruct((2 * block, rank), jnp.bfloat16), jax.ShapeDtypeStruct((1, rank), jnp.float32)],
        compiler_params=pltpu.CompilerParams(vmem_limit_bytes=ROOMY),
        name="times_inverse",
    )(first, second, high, low)


def momentum_kernel(which_ref, ids_ref, left_ref, back_ref, blended_ref, *refs):
    feedback = lax.dot_general(left_ref[...], back_ref[...], ROWS_BY_ROWS, preferred_element_type=jnp.float32)
    refs[-1][...] = (blended_ref[...].astype(jnp.float32) - (1.0 - momentum_decay) * feedback).astype(jnp.bfloat16)


def write_momentum(which, ids, left, back, blended, earlier):
    rows, rank = left.shape
    units = blended.shape[1]
    block = units // BLOCKS
    return pl.pallas_call(
        momentum_kernel,
        grid_spec=pltpu.PrefetchScalarGridSpec(
            num_scalar_prefetch=2,
            grid=(2,),
            in_specs=[
                fixed((rows, rank)),
                pl.BlockSpec((block, rank), lambda step, which_ref, ids_ref: (step, 0)),
                pl.BlockSpec((rows, block), lambda step, which_ref, ids_ref: (0, ids_ref[step])),
            ]
            + [pl.BlockSpec(memory_space=pl.ANY)] * len(earlier),
            out_specs=pl.BlockSpec((None, rows, block), lambda step, which_ref, ids_ref: (which_ref[0], 0, ids_ref[step])),
        ),
        out_shape=jax.ShapeDtypeStruct((2, rows, units), jnp.bfloat16),
        input_output_aliases={5: 0} if earlier else {},
        compiler_params=pltpu.CompilerParams(vmem_limit_bytes=ROOMY),
        name="write_momentum",
    )(which, ids, left, back, blended, *earlier)


def update_kernel(which_ref, ids_ref, *refs, scale):
    update_ref, basis_ref = refs[-2:]
    step = pl.program_id(0)

    def run(left_ref, back_ref, inverse_ref):
        normed = (back_ref[...].astype(jnp.float32) * inverse_ref[...]).astype(jnp.bfloat16)
        basis_ref[...] = normed
        product = lax.dot_general(left_ref[...], normed, ROWS_BY_ROWS, preferred_element_type=jnp.float32)
        update_ref[...] = (scale * product).astype(jnp.bfloat16)

    for part in range(4):
        left_ref, inverse_ref, *backs = refs[4 * (part // 2) : 4 * (part // 2) + 4]

        @pl.when(step // 2 == part)
        def _():
            run(left_ref, backs[part % 2], inverse_ref)


def write_updates(which, ids, own, other, scale):
    rows, rank = own[0].shape
    block = own[2].shape[0] // 2
    units = BLOCKS * block

    def piece(part):
        return pl.BlockSpec((block, rank), lambda step, *_: (jnp.clip(step - 2 * part, 0, 1), 0))

    specs = []
    for weight in range(2):
        specs += [fixed((rows, rank)), fixed((1, rank)), piece(2 * weight), piece(2 * weight + 1)]
    return pl.pallas_call(
        functools.partial(update_kernel, scale=scale),
        grid_spec=pltpu.PrefetchScalarGridSpec(
            num_scalar_prefetch=2,
            grid=(2 * BLOCKS,),
            in_specs=specs,
            out_specs=[
                pl.BlockSpec(
                    (None, rows, block),
                    lambda step, which_ref, ids_ref: (which_ref[step // BLOCKS], 0, ids_ref[step % BLOCKS]),
                ),
                pl.BlockSpec(
                    (None, block, rank),
                    lambda step, which_ref, ids_ref: (which_ref[step // BLOCKS], ids_ref[step % BLOCKS], 0),
                ),
            ],
        ),
        out_shape=[
            jax.ShapeDtypeStruct((2, rows, units), jnp.bfloat16),
            jax.ShapeDtypeStruct((2, units, rank), jnp.bfloat16),
        ],
        compiler_params=pltpu.CompilerParams(vmem_limit_bytes=ROOMY),
        name="write_updates",
    )(which, ids, *own, *other)


def swap(value, axis, bit, size):
    return lax.ppermute(value, axis, [(i, i ^ bit) for i in range(size)])


def bits_of(size):
    return [1 << i for i in range(size.bit_length() - 1)]


def added(first, second):
    return (first.astype(jnp.float32) + second.astype(jnp.float32)).astype(first.dtype)


def halved(value, axis, bit):
    high = (lax.axis_index(axis) & bit) != 0
    size = value.shape[0] // 2
    first, second = value[:size], value[size:]
    return jnp.where(high, second, first), jnp.where(high, first, second)


def joined(mine, theirs, axis, bit):
    high = (lax.axis_index(axis) & bit) != 0
    return jnp.where(high, jnp.concatenate([theirs, mine]), jnp.concatenate([mine, theirs]))


def after(value, *earlier):
    return lax.optimization_barrier((value, earlier))[0]


def butterfly(orders):
    steps = [(True, [order[i] for order in orders]) for i in range(len(orders[0]))]
    return steps + [(False, bits) for _, bits in reversed(steps)]


def outgoing(values, axis, step):
    reduces, bits = step
    return [halved(value, axis, bit) if reduces else (value, value) for value, bit in zip(values, bits)]


def sent(pairs, axis, size, step):
    return [swap(pair[1], axis, bit, size) for pair, bit in zip(pairs, step[1])]


def incoming(pairs, received, axis, step):
    reduces, bits = step
    return [
        added(pair[0], got) if reduces else joined(pair[0], got, axis, bit)
        for pair, got, bit in zip(pairs, received, bits)
    ]


def double_all(values, axis, size, orders):
    values = list(values)
    for step in range(len(orders[0])):
        for i, order in enumerate(orders):
            values[i] = added(values[i], swap(values[i], axis, order[step], size))
    return values


def shards(grads, momentum, basis, *, sizes):
    owner = lax.axis_index("replica")
    own = owner.astype(jnp.int32).reshape(1)
    other = 1 - own
    grads = grads[0]
    fsdp, tensor = sizes["fsdp"], sizes["tensor"]
    rank = basis.shape[-1]
    bits = bits_of(fsdp)
    orders = [bits, bits[::-1]]
    product = functools.partial(lax.dot_general, preferred_element_type=jnp.float32)
    switch = functools.partial(swap, axis="replica", bit=1, size=2)

    leaving, mine = partial_projection(own, grads, momentum, basis)
    summed = added(mine, switch(leaving))
    theirs = switch(after(grads, summed))

    def blend(which, tied):
        pick = functools.partial(lax.dynamic_index_in_dim, index=which, axis=0, keepdims=False)
        held, got = after((grads, theirs), tied)
        return (
            pick(momentum).astype(jnp.float32) + (pick(held).astype(jnp.float32) + pick(got).astype(jnp.float32))
        ).astype(jnp.bfloat16)

    values = [summed]
    steps = butterfly([bits_of(tensor)])
    blends = {len(steps) - 2: owner, len(steps) - 1: other[0]}
    blended = []
    for number, step in enumerate(steps):
        pairs = outgoing(values, "tensor", step)
        received = sent(pairs, "tensor", tensor, step)
        if number in blends:
            blended.append(blend(blends[number], [pair[1] for pair in pairs]))
            received = after(received, blended[-1])
        values = incoming(pairs, received, "tensor", step)
    projected = values[0]
    blended_own, blended_other = blended

    place = lax.axis_index("fsdp").astype(jnp.int32)
    ends = [jnp.where(place & order[0], 1, 0) for order in orders]
    held = jnp.stack([ends[0], 2 + ends[1]]).astype(jnp.int32)
    missing = jnp.stack([1 - ends[0], 3 - ends[1]]).astype(jnp.int32)

    gram = product(projected, projected, COLUMNS_BY_COLUMNS).astype(jnp.bfloat16)
    half = rank // 2
    grams = [gram[:half], gram[half:]]
    steps = butterfly(orders)
    send = cross(missing, blended_own, after(projected, grams))
    received = sent([(None, value) for value in send], "fsdp", fsdp, steps[0])
    keep = cross(held, blended_own, after(projected, send))
    work = after(jnp.concatenate(double_all(grams, "fsdp", fsdp, orders)), keep)
    todo = list(range(rank // LANES))
    turns = [2] + [1] * len(todo)
    pairs = list(zip(keep, send))
    for number, step in enumerate(steps):
        if number > 0:
            pairs = outgoing(values, "fsdp", step)
            received = sent(pairs, "fsdp", fsdp, step)
        for _ in range(min(turns[number] if number < len(turns) else 0, len(todo))):
            work = chol_step(after(work, [pair[1] for pair in pairs]), todo.pop(0), rank)
        received = after(received, work)
        if number == len(steps) - 1:
            break
        values = incoming(pairs, received, "fsdp", step)
    while todo:
        work = chol_step(work, todo.pop(0), rank)
    high, low = work

    high, low = after((high, low), values)
    half = projected.shape[0] // 2
    left, _ = times_inverse(projected[:half], projected[half:], high, low)
    back_held, squares_held = times_inverse(*values, high, low)
    left_other = switch(left)
    back_held_other = switch(back_held)
    momentum_new = write_momentum(own, held, left, back_held, blended_own, ())
    momentum_new = write_momentum(other, held, left_other, back_held_other, blended_other, (momentum_new,))

    received = after(received, momentum_new)
    back_got, squares_got = times_inverse(*received, high, low)
    back_got_other = switch(back_got)
    (squares,) = double_all([squares_held + squares_got], "tensor", tensor, [bits_of(tensor)])
    momentum_new = write_momentum(own, missing, left, back_got, blended_own, (momentum_new,))
    momentum_new = write_momentum(other, missing, left_other, back_got_other, blended_other, (momentum_new,))
    squares = after(squares, momentum_new)
    inverse = 1.0 / (jnp.sqrt(squares) + 1e-06)
    inverse_other = switch(inverse)

    scale = math.sqrt(grads.shape[1] * fsdp * grads.shape[2] * tensor / rank)
    update, basis_new = write_updates(
        jnp.concatenate([own, other]),
        jnp.concatenate([held, missing]),
        (left, inverse, back_held, back_got),
        (left_other, inverse_other, back_held_other, back_got_other),
        scale,
    )
    return (momentum_new, update, basis_new)


def solution(mesh):
    placed = (
        P("replica", None, "fsdp", "tensor"),
        P(None, "fsdp", "tensor"),
        P(None, "tensor", None),
    )
    return jax.shard_map(
        functools.partial(shards, sizes=dict(mesh.shape)),
        mesh=mesh,
        in_specs=placed,
        out_specs=(P(None, "fsdp", "tensor"), P(None, "fsdp", "tensor"), P(None, "tensor", None)),
        check_vma=False,
    )
```

```python
import functools
import math

import jax
import jax.numpy as jnp
from jax import lax
from jax.experimental import pallas as pl
from jax.experimental.pallas import tpu as pltpu
from jax.sharding import PartitionSpec as P

LANES = 128
SUBS = 8
BLOCKS = 4
momentum_decay = 0.95


def invert_block(rows):
    count = len(rows)
    lane = lax.broadcasted_iota(jnp.int32, (SUBS, LANES), 1)
    sub = lax.broadcasted_iota(jnp.int32, (SUBS, LANES), 0)
    rows = list(rows)
    wide = lambda v, i: jnp.broadcast_to(v[i:i+1, :], (SUBS, LANES))
    col = lambda v, c: jnp.broadcast_to(v[:, c:c+1], (SUBS, LANES))
    for p in range(count):
        base = p * SUBS
        inside = (lane >= base) & (lane < base + SUBS)
        mine = rows[p]
        cols = [col(mine, base + i) for i in range(SUBS)]
        solved = jnp.where(inside, jnp.where(lane == base + sub, 1.0, 0.0), mine)
        half = solved
        for i in range(SUBS):
            pivot = wide(cols[i], i)
            inverse = 1.0 / pivot
            at = sub == i
            gain = jnp.where(at, 1.0 - inverse, cols[i] * inverse)
            for j in range(i + 1, SUBS):
                cols[j] = cols[j] - gain * wide(cols[j], i)
            row = wide(solved, i)
            half = jnp.where(at, row * lax.rsqrt(pivot), half)
            solved = solved - gain * row
        rows[p] = jnp.where(lane < base + SUBS, half, 0.0)
        if p + 1 < count:
            wides = [wide(solved, i) for i in range(SUBS)]
            for q in range(p + 1, count):
                below = rows[q]
                terms = [col(below, base + i) * wides[i] for i in range(SUBS)]
                while len(terms) > 1:
                    terms = [a + b for a, b in zip(terms[::2], terms[1::2])]
                rows[q] = jnp.where(inside, 0.0, below) - terms[0]
    return rows


def chol_kernel(*refs, k, blocks):
    last = k == blocks - 1
    source, part = refs[0], refs[-1]
    work = refs[1]
    if k == 0:
        for c in range(blocks):
            work[c] = source[:, c * LANES : (c + 1) * LANES].astype(jnp.float32)
        held = work
    else:
        held = source
    dot = functools.partial(lax.dot_general, preferred_element_type=jnp.float32, precision=lax.Precision.HIGHEST)
    start = k * LANES
    mine = slice(start, start + LANES)
    inv = jnp.concatenate(
        invert_block([held[k, start + SUBS * q : start + SUBS * (q + 1), :] for q in range(LANES // SUBS)]), axis=0
    )
    for c in range(blocks):
        part[c] = inv if c == k else dot(inv, held[c, mine, :], (((1,), (0,)), ((), ())))
    if not last:
        for c in range(blocks):
            if k > 0:
                work[c, :start, :] = held[c, :start, :]
            work[c, mine, :] = part[c]
        for r in range(k + 1, blocks):
            rows = slice(r * LANES, (r + 1) * LANES)
            for c in range(blocks):
                if c > k and c < r:
                    continue
                product = dot(part[r], part[c], (((0,), (0,)), ((), ())))
                work[c, rows, :] = -product if c == k else held[c, rows, :] - product
        return
    high_ref, low_ref = refs[1:3]
    for r in range(blocks):
        rows = slice(r * LANES, (r + 1) * LANES)
        for c in range(blocks):
            cut = slice(c * LANES, (c + 1) * LANES)
            if c > r:
                high_ref[rows, cut] = jnp.zeros((LANES, LANES), jnp.bfloat16)
                low_ref[rows, cut] = jnp.zeros((LANES, LANES), jnp.bfloat16)
                continue
            value = part[c] if r == k else held[c, rows, :]
            high = value.astype(jnp.bfloat16)
            high_ref[rows, cut] = high
            low_ref[rows, cut] = (value - high.astype(jnp.float32)).astype(jnp.bfloat16)


def chol_step(value, k, size):
    blocks = size // LANES
    if k == blocks - 1:
        out_shape = [jax.ShapeDtypeStruct((size, size), jnp.bfloat16)] * 2
    else:
        out_shape = [jax.ShapeDtypeStruct((blocks, size, LANES), jnp.float32)]
    results = pl.pallas_call(
        functools.partial(chol_kernel, k=k, blocks=blocks),
        out_shape=out_shape,
        in_specs=[pl.BlockSpec(memory_space=pltpu.VMEM)],
        out_specs=[pl.BlockSpec(memory_space=pltpu.VMEM)] * len(out_shape),
        scratch_shapes=[pltpu.VMEM((blocks, LANES, LANES), jnp.float32)],
        compiler_params=pltpu.CompilerParams(vmem_limit_bytes=16 << 20),
        name="chol_step",
    )(value)
    return results if k == blocks - 1 else results[0]


def partial_kernel(which_ref, grads_ref, moment_ref, basis_ref, sent_ref, mine_ref):
    @pl.when(pl.program_id(0) == 0)
    def _():
        sent_ref[...] = jnp.dot(grads_ref[...], basis_ref[...], preferred_element_type=jnp.float32).astype(jnp.bfloat16)

    @pl.when(pl.program_id(0) == 1)
    def _():
        rows = (grads_ref[...].astype(jnp.float32) + moment_ref[...].astype(jnp.float32)).astype(jnp.bfloat16)
        mine_ref[...] = jnp.dot(rows, basis_ref[...], preferred_element_type=jnp.float32).astype(jnp.bfloat16)


def partial_projection(own, grads, moment, basis):
    _, rows, units = grads.shape
    rank = basis.shape[-1]
    parts = 2
    tile = rows // parts

    def weight_of(weight, own_ref):
        return jnp.where(weight == 0, 1 - own_ref[0], own_ref[0])

    return pl.pallas_call(
        partial_kernel,
        grid_spec=pltpu.PrefetchScalarGridSpec(
            num_scalar_prefetch=1,
            grid=(2, parts),
            in_specs=[
                pl.BlockSpec((None, tile, units), lambda weight, step, own_ref: (weight_of(weight, own_ref), step, 0)),
                pl.BlockSpec((None, tile, units), lambda weight, step, own_ref: (own_ref[0], step * weight, 0)),
                pl.BlockSpec((None, units, rank), lambda weight, step, own_ref: (weight_of(weight, own_ref), 0, 0)),
            ],
            out_specs=[
                pl.BlockSpec((tile, rank), lambda weight, step, own_ref: (jnp.where(weight == 0, step, parts - 1), 0)),
                pl.BlockSpec((tile, rank), lambda weight, step, own_ref: (step * weight, 0)),
            ],
        ),
        out_shape=[jax.ShapeDtypeStruct((rows, rank), jnp.bfloat16)] * 2,
        compiler_params=pltpu.CompilerParams(vmem_limit_bytes=ROOMY),
        name="partial_projection",
    )(own, grads, moment, basis)


ROWS_BY_ROWS = (((1,), (1,)), ((), ()))
COLUMNS_BY_COLUMNS = (((0,), (0,)), ((), ()))
ROOMY = 48 << 20


def fixed(shape):
    return pl.BlockSpec(shape, lambda step, *_: (0,) * len(shape))


def cross_kernel(ids_ref, blended_ref, projected_ref, first_ref, second_ref):
    product = lax.dot_general(
        blended_ref[...], projected_ref[...], COLUMNS_BY_COLUMNS, preferred_element_type=jnp.float32
    ).astype(jnp.bfloat16)
    for step, ref in enumerate((first_ref, second_ref)):

        @pl.when(pl.program_id(0) == step)
        def _():
            ref[...] = product


def cross(ids, blended, projected):
    rows, rank = projected.shape
    block = blended.shape[1] // BLOCKS
    return pl.pallas_call(
        cross_kernel,
        grid_spec=pltpu.PrefetchScalarGridSpec(
            num_scalar_prefetch=1,
            grid=(2,),
            in_specs=[pl.BlockSpec((rows, block), lambda step, ids_ref: (0, ids_ref[step])), fixed((rows, rank))],
            out_specs=[fixed((block, rank))] * 2,
        ),
        out_shape=[jax.ShapeDtypeStruct((block, rank), jnp.bfloat16)] * 2,
        compiler_params=pltpu.CompilerParams(vmem_limit_bytes=ROOMY),
        name="cross",
    )(ids, blended, projected)


def back_kernel(first_ref, second_ref, high_ref, low_ref, back_ref, squares_ref):
    step = pl.program_id(0)

    def run(ref):
        rows = ref[...]
        back = lax.dot_general(rows, high_ref[...], ROWS_BY_ROWS, preferred_element_type=jnp.float32)
        back += lax.dot_general(rows, low_ref[...], ROWS_BY_ROWS, preferred_element_type=jnp.float32)
        back_ref[...] = back.astype(jnp.bfloat16)
        return jnp.sum(back * back, axis=0, keepdims=True)

    @pl.when(step == 0)
    def _():
        squares_ref[...] = run(first_ref)

    @pl.when(step == 1)
    def _():
        squares_ref[...] += run(second_ref)


def times_inverse(first, second, high, low):
    block, rank = first.shape
    return pl.pallas_call(
        back_kernel,
        grid=(2,),
        in_specs=[fixed((block, rank))] * 2 + [fixed((rank, rank))] * 2,
        out_specs=[pl.BlockSpec((block, rank), lambda step: (step, 0)), fixed((1, rank))],
        out_shape=[jax.ShapeDtypeStruct((2 * block, rank), jnp.bfloat16), jax.ShapeDtypeStruct((1, rank), jnp.float32)],
        compiler_params=pltpu.CompilerParams(vmem_limit_bytes=ROOMY),
        name="times_inverse",
    )(first, second, high, low)


def new_momentum(left_ref, back_ref, blended_ref):
    feedback = lax.dot_general(left_ref[...], back_ref[...], ROWS_BY_ROWS, preferred_element_type=jnp.float32)
    return (blended_ref[...].astype(jnp.float32) - (1.0 - momentum_decay) * feedback).astype(jnp.bfloat16)


def momentum_kernel(which_ref, ids_ref, *refs, weights):
    for weight in range(weights):

        @pl.when(pl.program_id(0) // 2 == weight)
        def _():
            refs[-1][...] = new_momentum(*refs[3 * weight : 3 * weight + 3])


def write_momentum(which, ids, operands, earlier):
    rows, rank = operands[0][0].shape
    units = operands[0][2].shape[1]
    block = units // BLOCKS
    specs = []
    for weight in range(len(operands)):

        def local(step, weight=weight):
            return jnp.clip(step - 2 * weight, 0, 1)

        specs += [
            fixed((rows, rank)),
            pl.BlockSpec((block, rank), lambda step, which_ref, ids_ref, local=local: (local(step), 0)),
            pl.BlockSpec((rows, block), lambda step, which_ref, ids_ref, local=local: (0, ids_ref[local(step)])),
        ]
    flat = [value for group in operands for value in group]
    return pl.pallas_call(
        functools.partial(momentum_kernel, weights=len(operands)),
        grid_spec=pltpu.PrefetchScalarGridSpec(
            num_scalar_prefetch=2,
            grid=(2 * len(operands),),
            in_specs=specs + [pl.BlockSpec(memory_space=pl.ANY)] * len(earlier),
            out_specs=pl.BlockSpec(
                (None, rows, block), lambda step, which_ref, ids_ref: (which_ref[step // 2], 0, ids_ref[step % 2])
            ),
        ),
        out_shape=jax.ShapeDtypeStruct((2, rows, units), jnp.bfloat16),
        input_output_aliases={2 + len(flat): 0} if earlier else {},
        compiler_params=pltpu.CompilerParams(vmem_limit_bytes=ROOMY),
        name="write_momentum",
    )(which, ids, *flat, *earlier)


def final_kernel(which_ref, ids_ref, *refs, scale):
    blended_ref = refs[8]
    momentum_ref, update_ref, basis_ref = refs[-3:]
    step = pl.program_id(0)

    for part in range(4):
        left_ref, inverse_ref, *backs = refs[4 * (part // 2) : 4 * (part // 2) + 4]
        back_ref = backs[part % 2]

        @pl.when(step // 2 == part)
        def _():
            normed = (back_ref[...].astype(jnp.float32) * inverse_ref[...]).astype(jnp.bfloat16)
            basis_ref[...] = normed
            product = lax.dot_general(left_ref[...], normed, ROWS_BY_ROWS, preferred_element_type=jnp.float32)
            update_ref[...] = (scale * product).astype(jnp.bfloat16)
            if part >= 2:
                momentum_ref[...] = new_momentum(left_ref, back_ref, blended_ref)


def write_final(which, ids, own, other, blended, momentum_new, scale):
    rows, rank = own[0].shape
    block = own[2].shape[0] // 2
    units = BLOCKS * block

    def piece(part):
        return pl.BlockSpec((block, rank), lambda step, *_: (jnp.clip(step - 2 * part, 0, 1), 0))

    def late(step):
        return jnp.maximum(step - BLOCKS, 0)

    specs = []
    for weight in range(2):
        specs += [fixed((rows, rank)), fixed((1, rank)), piece(2 * weight), piece(2 * weight + 1)]
    specs.append(pl.BlockSpec((rows, block), lambda step, which_ref, ids_ref: (0, ids_ref[late(step)])))
    specs.append(pl.BlockSpec(memory_space=pl.ANY))
    return pl.pallas_call(
        functools.partial(final_kernel, scale=scale),
        grid_spec=pltpu.PrefetchScalarGridSpec(
            num_scalar_prefetch=2,
            grid=(2 * BLOCKS,),
            in_specs=specs,
            out_specs=[
                pl.BlockSpec(
                    (None, rows, block), lambda step, which_ref, ids_ref: (which_ref[1], 0, ids_ref[late(step)])
                ),
                pl.BlockSpec(
                    (None, rows, block),
                    lambda step, which_ref, ids_ref: (which_ref[step // BLOCKS], 0, ids_ref[step % BLOCKS]),
                ),
                pl.BlockSpec(
                    (None, block, rank),
                    lambda step, which_ref, ids_ref: (which_ref[step // BLOCKS], ids_ref[step % BLOCKS], 0),
                ),
            ],
        ),
        out_shape=[
            jax.ShapeDtypeStruct((2, rows, units), jnp.bfloat16),
            jax.ShapeDtypeStruct((2, rows, units), jnp.bfloat16),
            jax.ShapeDtypeStruct((2, units, rank), jnp.bfloat16),
        ],
        input_output_aliases={11: 0},
        compiler_params=pltpu.CompilerParams(vmem_limit_bytes=ROOMY),
        name="write_final",
    )(which, ids, *own, *other, blended, momentum_new)


def swap(value, axis, bit, size):
    return lax.ppermute(value, axis, [(i, i ^ bit) for i in range(size)])


def bits_of(size):
    return [1 << i for i in range(size.bit_length() - 1)]


def added(first, second):
    return (first.astype(jnp.float32) + second.astype(jnp.float32)).astype(first.dtype)


def halved(value, axis, bit):
    high = (lax.axis_index(axis) & bit) != 0
    size = value.shape[0] // 2
    first, second = value[:size], value[size:]
    return jnp.where(high, second, first), jnp.where(high, first, second)


def joined(mine, theirs, axis, bit):
    high = (lax.axis_index(axis) & bit) != 0
    return jnp.where(high, jnp.concatenate([theirs, mine]), jnp.concatenate([mine, theirs]))


def after(value, *earlier):
    return lax.optimization_barrier((value, earlier))[0]


def butterfly(orders):
    steps = [(True, [order[i] for order in orders]) for i in range(len(orders[0]))]
    return steps + [(False, bits) for _, bits in reversed(steps)]


def outgoing(values, axis, step):
    reduces, bits = step
    return [halved(value, axis, bit) if reduces else (value, value) for value, bit in zip(values, bits)]


def sent(pairs, axis, size, step):
    return [swap(pair[1], axis, bit, size) for pair, bit in zip(pairs, step[1])]


def incoming(pairs, received, axis, step):
    reduces, bits = step
    return [
        added(pair[0], got) if reduces else joined(pair[0], got, axis, bit)
        for pair, got, bit in zip(pairs, received, bits)
    ]


def offsets(size):
    return sorted(range(1, size), reverse=True)


def scatter_sum(value, axis, size):
    place = lax.axis_index(axis)
    pieces = value.reshape(size, value.shape[0] // size, value.shape[1])
    pick = functools.partial(lax.dynamic_index_in_dim, axis=0, keepdims=False)
    return pick(pieces, place), [swap(pick(pieces, place ^ d), axis, d, size) for d in offsets(size)]


def sum_of(mine, arrived):
    total = mine.astype(jnp.float32)
    for value in arrived:
        total += value.astype(jnp.float32)
    return total


def gather_rows(mine, arrived, axis, size):
    place = lax.axis_index(axis)
    slots = [mine] + [None] * (size - 1)
    for d, value in zip(offsets(size), arrived):
        slots[d] = value
    slots = jnp.stack(slots)
    return jnp.concatenate(
        [lax.dynamic_index_in_dim(slots, place ^ j, axis=0, keepdims=False) for j in range(size)]
    )


def shards(grads, momentum, basis, *, sizes):
    owner = lax.axis_index("replica")
    own = owner.astype(jnp.int32).reshape(1)
    other = 1 - own
    grads = grads[0]
    fsdp, tensor = sizes["fsdp"], sizes["tensor"]
    rank = basis.shape[-1]
    bits = bits_of(fsdp)
    orders = [bits, bits[::-1]]
    product = functools.partial(lax.dot_general, preferred_element_type=jnp.float32)
    switch = functools.partial(swap, axis="replica", bit=1, size=2)

    leaving, mine = partial_projection(own, grads, momentum, basis)
    summed = added(mine, switch(leaving))
    theirs = switch(after(grads, summed))

    def blend(which, tied):
        pick = functools.partial(lax.dynamic_index_in_dim, index=which, axis=0, keepdims=False)
        held, got = after((grads, theirs), tied)
        return (
            pick(momentum).astype(jnp.float32) + (pick(held).astype(jnp.float32) + pick(got).astype(jnp.float32))
        ).astype(jnp.bfloat16)

    keep, arrived = scatter_sum(summed, "tensor", tensor)
    piece = sum_of(keep, arrived).astype(jnp.bfloat16)
    arrived = [swap(piece, "tensor", d, tensor) for d in offsets(tensor)]
    blended_own = blend(owner, piece)
    arrived = after(arrived, blended_own)
    projected = gather_rows(piece, arrived, "tensor", tensor)

    place = lax.axis_index("fsdp").astype(jnp.int32)
    ends = [jnp.where(place & order[0], 1, 0) for order in orders]
    held = jnp.stack([ends[0], 2 + ends[1]]).astype(jnp.int32)
    missing = jnp.stack([1 - ends[0], 3 - ends[1]]).astype(jnp.int32)

    gram = product(projected, projected, COLUMNS_BY_COLUMNS).astype(jnp.bfloat16)
    half = rank // 2
    grams = [gram[:half], gram[half:]]
    send = keep = None
    for number in range(len(bits)):
        received = [swap(value, "fsdp", order[number], fsdp) for value, order in zip(grams, orders)]
        if number == 0:
            send = cross(missing, blended_own, after(projected, grams))
            received = after(received, send)
        if number == 1:
            keep = cross(held, blended_own, after(projected, grams, send))
            received = after(received, keep)
        grams = [added(value, got) for value, got in zip(grams, received)]
    work = jnp.concatenate(grams)
    steps = butterfly(orders)
    send = after(send, work)
    received = sent([(None, value) for value in send], "fsdp", fsdp, steps[0])
    todo = list(range(rank // LANES))
    turns = [3] + [1] * len(todo)
    pairs = list(zip(keep, send))
    for number, step in enumerate(steps):
        if number > 0:
            pairs = outgoing(values, "fsdp", step)
            received = sent(pairs, "fsdp", fsdp, step)
        for _ in range(min(turns[number] if number < len(turns) else 0, len(todo))):
            work = chol_step(after(work, [pair[1] for pair in pairs]), todo.pop(0), rank)
        received = after(received, work)
        if number == len(steps) - 1:
            break
        if number == len(steps) - 2:
            while todo:
                work = chol_step(work, todo.pop(0), rank)
            high, low = work
            half = projected.shape[0] // 2
            left, _ = times_inverse(*after((projected[:half], projected[half:]), [pair[1] for pair in pairs]), high, low)
            received = after(received, left)
        values = incoming(pairs, received, "fsdp", step)

    both = jnp.concatenate([own, other])
    back_held, squares_held = times_inverse(*after(values, left), high, low)
    momentum_new = write_momentum(own, held, [(left, back_held, blended_own)], ())
    blended_other = blend(other[0], (values, back_held))
    received = after(received, (momentum_new, blended_other))
    left_other = switch(after(left, received))
    back_held_other = switch(after(back_held, received))
    back_got, squares_got = times_inverse(*received, high, low)
    back_got_other = switch(back_got)
    local = squares_held + squares_got
    arrived = [swap(local, "tensor", d, tensor) for d in offsets(tensor)]
    momentum_new = write_momentum(own, missing, [(left, after(back_got, local), blended_own)], (momentum_new,))
    squares = sum_of(local, after(arrived, momentum_new))
    inverse = 1.0 / (jnp.sqrt(squares) + 1e-06)
    inverse_other = switch(inverse)

    scale = math.sqrt(grads.shape[1] * fsdp * grads.shape[2] * tensor / rank)
    return tuple(
        write_final(
            both,
            jnp.concatenate([held, missing]),
            (left, inverse, back_held, back_got),
            (left_other, inverse_other, back_held_other, back_got_other),
            blended_other,
            momentum_new,
            scale,
        )
    )


def solution(mesh):
    placed = (
        P("replica", None, "fsdp", "tensor"),
        P(None, "fsdp", "tensor"),
        P(None, "tensor", None),
    )
    return jax.shard_map(
        functools.partial(shards, sizes=dict(mesh.shape)),
        mesh=mesh,
        in_specs=placed,
        out_specs=(P(None, "fsdp", "tensor"), P(None, "fsdp", "tensor"), P(None, "tensor", None)),
        check_vma=False,
    )
```

```python
import functools
import math

import jax
import jax.numpy as jnp
from jax import lax
from jax.experimental import pallas as pl
from jax.experimental.pallas import tpu as pltpu
from jax.sharding import PartitionSpec as P

LANES = 128
SUBS = 8
BLOCKS = 4
momentum_decay = 0.95


def invert_block(rows):
    count = len(rows)
    lane = lax.broadcasted_iota(jnp.int32, (SUBS, LANES), 1)
    sub = lax.broadcasted_iota(jnp.int32, (SUBS, LANES), 0)
    rows = list(rows)
    wide = lambda v, i: jnp.broadcast_to(v[i:i+1, :], (SUBS, LANES))
    col = lambda v, c: jnp.broadcast_to(v[:, c:c+1], (SUBS, LANES))
    for p in range(count):
        base = p * SUBS
        inside = (lane >= base) & (lane < base + SUBS)
        mine = rows[p]
        cols = [col(mine, base + i) for i in range(SUBS)]
        solved = jnp.where(inside, jnp.where(lane == base + sub, 1.0, 0.0), mine)
        half = solved
        for i in range(SUBS):
            pivot = wide(cols[i], i)
            inverse = 1.0 / pivot
            at = sub == i
            gain = jnp.where(at, 1.0 - inverse, cols[i] * inverse)
            for j in range(i + 1, SUBS):
                cols[j] = cols[j] - gain * wide(cols[j], i)
            row = wide(solved, i)
            half = jnp.where(at, row * lax.rsqrt(pivot), half)
            solved = solved - gain * row
        rows[p] = jnp.where(lane < base + SUBS, half, 0.0)
        if p + 1 < count:
            wides = [wide(solved, i) for i in range(SUBS)]
            for q in range(p + 1, count):
                below = rows[q]
                terms = [col(below, base + i) * wides[i] for i in range(SUBS)]
                while len(terms) > 1:
                    terms = [a + b for a, b in zip(terms[::2], terms[1::2])]
                rows[q] = jnp.where(inside, 0.0, below) - terms[0]
    return rows


def chol_kernel(*refs, k, blocks):
    last = k == blocks - 1
    source, part = refs[0], refs[-1]
    work = refs[1]
    if k == 0:
        for c in range(blocks):
            work[c] = source[:, c * LANES : (c + 1) * LANES].astype(jnp.float32)
        held = work
    else:
        held = source
    dot = functools.partial(lax.dot_general, preferred_element_type=jnp.float32, precision=lax.Precision.HIGHEST)
    start = k * LANES
    mine = slice(start, start + LANES)
    inv = jnp.concatenate(
        invert_block([held[k, start + SUBS * q : start + SUBS * (q + 1), :] for q in range(LANES // SUBS)]), axis=0
    )
    for c in range(blocks):
        part[c] = inv if c == k else dot(inv, held[c, mine, :], (((1,), (0,)), ((), ())))
    if not last:
        for c in range(blocks):
            if k > 0:
                work[c, :start, :] = held[c, :start, :]
            work[c, mine, :] = part[c]
        for r in range(k + 1, blocks):
            rows = slice(r * LANES, (r + 1) * LANES)
            for c in range(blocks):
                if c > k and c < r:
                    continue
                product = dot(part[r], part[c], (((0,), (0,)), ((), ())))
                work[c, rows, :] = -product if c == k else held[c, rows, :] - product
        return
    high_ref, low_ref = refs[1:3]
    for r in range(blocks):
        rows = slice(r * LANES, (r + 1) * LANES)
        for c in range(blocks):
            cut = slice(c * LANES, (c + 1) * LANES)
            if c > r:
                high_ref[rows, cut] = jnp.zeros((LANES, LANES), jnp.bfloat16)
                low_ref[rows, cut] = jnp.zeros((LANES, LANES), jnp.bfloat16)
                continue
            value = part[c] if r == k else held[c, rows, :]
            high = value.astype(jnp.bfloat16)
            high_ref[rows, cut] = high
            low_ref[rows, cut] = (value - high.astype(jnp.float32)).astype(jnp.bfloat16)


def chol_step(value, k, size):
    blocks = size // LANES
    if k == blocks - 1:
        out_shape = [jax.ShapeDtypeStruct((size, size), jnp.bfloat16)] * 2
    else:
        out_shape = [jax.ShapeDtypeStruct((blocks, size, LANES), jnp.float32)]
    results = pl.pallas_call(
        functools.partial(chol_kernel, k=k, blocks=blocks),
        out_shape=out_shape,
        in_specs=[pl.BlockSpec(memory_space=pltpu.VMEM)],
        out_specs=[pl.BlockSpec(memory_space=pltpu.VMEM)] * len(out_shape),
        scratch_shapes=[pltpu.VMEM((blocks, LANES, LANES), jnp.float32)],
        compiler_params=pltpu.CompilerParams(vmem_limit_bytes=16 << 20),
        name="chol_step",
    )(value)
    return results if k == blocks - 1 else results[0]


def partial_kernel(which_ref, grads_ref, moment_ref, basis_ref, sent_ref, mine_ref):
    @pl.when(pl.program_id(0) == 0)
    def _():
        sent_ref[...] = jnp.dot(grads_ref[...], basis_ref[...], preferred_element_type=jnp.float32).astype(jnp.bfloat16)

    @pl.when(pl.program_id(0) == 1)
    def _():
        rows = (grads_ref[...].astype(jnp.float32) + moment_ref[...].astype(jnp.float32)).astype(jnp.bfloat16)
        mine_ref[...] = jnp.dot(rows, basis_ref[...], preferred_element_type=jnp.float32).astype(jnp.bfloat16)


def partial_projection(own, grads, moment, basis):
    _, rows, units = grads.shape
    rank = basis.shape[-1]
    parts = 2
    tile = rows // parts

    def weight_of(weight, own_ref):
        return jnp.where(weight == 0, 1 - own_ref[0], own_ref[0])

    return pl.pallas_call(
        partial_kernel,
        grid_spec=pltpu.PrefetchScalarGridSpec(
            num_scalar_prefetch=1,
            grid=(2, parts),
            in_specs=[
                pl.BlockSpec((None, tile, units), lambda weight, step, own_ref: (weight_of(weight, own_ref), step, 0)),
                pl.BlockSpec((None, tile, units), lambda weight, step, own_ref: (own_ref[0], step * weight, 0)),
                pl.BlockSpec((None, units, rank), lambda weight, step, own_ref: (weight_of(weight, own_ref), 0, 0)),
            ],
            out_specs=[
                pl.BlockSpec((tile, rank), lambda weight, step, own_ref: (jnp.where(weight == 0, step, parts - 1), 0)),
                pl.BlockSpec((tile, rank), lambda weight, step, own_ref: (step * weight, 0)),
            ],
        ),
        out_shape=[jax.ShapeDtypeStruct((rows, rank), jnp.bfloat16)] * 2,
        compiler_params=pltpu.CompilerParams(vmem_limit_bytes=ROOMY),
        name="partial_projection",
    )(own, grads, moment, basis)


ROWS_BY_ROWS = (((1,), (1,)), ((), ()))
COLUMNS_BY_COLUMNS = (((0,), (0,)), ((), ()))
ROOMY = 48 << 20


def fixed(shape):
    return pl.BlockSpec(shape, lambda step, *_: (0,) * len(shape))


def cross_kernel(ids_ref, blended_ref, projected_ref, first_ref, second_ref):
    product = lax.dot_general(
        blended_ref[...], projected_ref[...], COLUMNS_BY_COLUMNS, preferred_element_type=jnp.float32
    ).astype(jnp.bfloat16)
    for step, ref in enumerate((first_ref, second_ref)):

        @pl.when(pl.program_id(0) == step)
        def _():
            ref[...] = product


def cross(ids, blended, projected):
    rows, rank = projected.shape
    block = blended.shape[1] // BLOCKS
    return pl.pallas_call(
        cross_kernel,
        grid_spec=pltpu.PrefetchScalarGridSpec(
            num_scalar_prefetch=1,
            grid=(2,),
            in_specs=[pl.BlockSpec((rows, block), lambda step, ids_ref: (0, ids_ref[step])), fixed((rows, rank))],
            out_specs=[fixed((block, rank))] * 2,
        ),
        out_shape=[jax.ShapeDtypeStruct((block, rank), jnp.bfloat16)] * 2,
        compiler_params=pltpu.CompilerParams(vmem_limit_bytes=ROOMY),
        name="cross",
    )(ids, blended, projected)


def back_kernel(first_ref, second_ref, high_ref, low_ref, back_ref, squares_ref):
    step = pl.program_id(0)

    def run(ref):
        rows = ref[...]
        back = lax.dot_general(rows, high_ref[...], ROWS_BY_ROWS, preferred_element_type=jnp.float32)
        back += lax.dot_general(rows, low_ref[...], ROWS_BY_ROWS, preferred_element_type=jnp.float32)
        back_ref[...] = back.astype(jnp.bfloat16)
        return jnp.sum(back * back, axis=0, keepdims=True)

    @pl.when(step == 0)
    def _():
        squares_ref[...] = run(first_ref)

    @pl.when(step == 1)
    def _():
        squares_ref[...] += run(second_ref)


def times_inverse(first, second, high, low):
    block, rank = first.shape
    return pl.pallas_call(
        back_kernel,
        grid=(2,),
        in_specs=[fixed((block, rank))] * 2 + [fixed((rank, rank))] * 2,
        out_specs=[pl.BlockSpec((block, rank), lambda step: (step, 0)), fixed((1, rank))],
        out_shape=[jax.ShapeDtypeStruct((2 * block, rank), jnp.bfloat16), jax.ShapeDtypeStruct((1, rank), jnp.float32)],
        compiler_params=pltpu.CompilerParams(vmem_limit_bytes=ROOMY),
        name="times_inverse",
    )(first, second, high, low)


def write_kernel(which_ref, ids_ref, *refs, groups, scale):
    momentum_ref, update_ref, basis_ref = refs[-3:]
    for group in range(groups):
        left_ref, back_ref, blended_ref, inverse_ref = refs[4 * group : 4 * (group + 1)]

        @pl.when(pl.program_id(0) // 2 == group)
        def _():
            feedback = lax.dot_general(left_ref[...], back_ref[...], ROWS_BY_ROWS, preferred_element_type=jnp.float32)
            momentum_ref[...] = (
                blended_ref[...].astype(jnp.float32) - (1.0 - momentum_decay) * feedback
            ).astype(jnp.bfloat16)
            normed = (back_ref[...].astype(jnp.float32) * inverse_ref[...]).astype(jnp.bfloat16)
            basis_ref[...] = normed
            product = lax.dot_general(left_ref[...], normed, ROWS_BY_ROWS, preferred_element_type=jnp.float32)
            update_ref[...] = (scale * product).astype(jnp.bfloat16)


def write(which, ids, groups, earlier, scale):
    rows, rank = groups[0][0].shape
    block = groups[0][1].shape[0] // 2
    units = BLOCKS * block
    specs = []
    for group in range(len(groups)):

        def local(step, group=group):
            return jnp.clip(step - 2 * group, 0, 1)

        specs += [
            fixed((rows, rank)),
            pl.BlockSpec((block, rank), lambda step, w, i, local=local: (local(step), 0)),
            pl.BlockSpec((rows, block), lambda step, w, i, local=local, group=group: (0, i[2 * group + local(step)])),
            fixed((1, rank)),
        ]
    columns = pl.BlockSpec((None, rows, block), lambda step, w, i: (w[step // 2], 0, i[step]))
    wide = jax.ShapeDtypeStruct((2, rows, units), jnp.bfloat16)
    out_specs = [columns, columns, pl.BlockSpec((None, block, rank), lambda step, w, i: (w[step // 2], i[step], 0))]
    out_shape = [wide, wide, jax.ShapeDtypeStruct((2, units, rank), jnp.bfloat16)]
    flat = [value for group in groups for value in group]
    return pl.pallas_call(
        functools.partial(write_kernel, groups=len(groups), scale=scale),
        grid_spec=pltpu.PrefetchScalarGridSpec(
            num_scalar_prefetch=2,
            grid=(2 * len(groups),),
            in_specs=specs + [pl.BlockSpec(memory_space=pl.ANY)] * len(earlier),
            out_specs=out_specs,
        ),
        out_shape=out_shape,
        input_output_aliases={2 + len(flat) + i: i for i in range(len(earlier))},
        compiler_params=pltpu.CompilerParams(vmem_limit_bytes=ROOMY),
        name="write",
    )(which, ids, *flat, *earlier)


def swap(value, axis, bit, size):
    return lax.ppermute(value, axis, [(i, i ^ bit) for i in range(size)])


def bits_of(size):
    return [1 << i for i in range(size.bit_length() - 1)]


def added(first, second):
    return (first.astype(jnp.float32) + second.astype(jnp.float32)).astype(first.dtype)


def halved(value, axis, bit):
    high = (lax.axis_index(axis) & bit) != 0
    size = value.shape[0] // 2
    first, second = value[:size], value[size:]
    return jnp.where(high, second, first), jnp.where(high, first, second)


def joined(mine, theirs, axis, bit):
    high = (lax.axis_index(axis) & bit) != 0
    return jnp.where(high, jnp.concatenate([theirs, mine]), jnp.concatenate([mine, theirs]))


def after(value, *earlier):
    return lax.optimization_barrier((value, earlier))[0]


def butterfly(orders):
    steps = [(True, [order[i] for order in orders]) for i in range(len(orders[0]))]
    return steps + [(False, bits) for _, bits in reversed(steps)]


def outgoing(values, axis, step):
    reduces, bits = step
    return [halved(value, axis, bit) if reduces else (value, value) for value, bit in zip(values, bits)]


def sent(pairs, axis, size, step):
    return [swap(pair[1], axis, bit, size) for pair, bit in zip(pairs, step[1])]


def incoming(pairs, received, axis, step):
    reduces, bits = step
    return [
        added(pair[0], got) if reduces else joined(pair[0], got, axis, bit)
        for pair, got, bit in zip(pairs, received, bits)
    ]


def offsets(size):
    return sorted(range(1, size), reverse=True)


def scatter_sum(value, axis, size):
    place = lax.axis_index(axis)
    pieces = value.reshape(size, value.shape[0] // size, value.shape[1])
    pick = functools.partial(lax.dynamic_index_in_dim, axis=0, keepdims=False)
    return pick(pieces, place), [swap(pick(pieces, place ^ d), axis, d, size) for d in offsets(size)]


def sum_of(mine, arrived):
    total = mine.astype(jnp.float32)
    for value in arrived:
        total += value.astype(jnp.float32)
    return total


def gather_rows(mine, arrived, axis, size):
    place = lax.axis_index(axis)
    slots = [mine] + [None] * (size - 1)
    for d, value in zip(offsets(size), arrived):
        slots[d] = value
    slots = jnp.stack(slots)
    return jnp.concatenate(
        [lax.dynamic_index_in_dim(slots, place ^ j, axis=0, keepdims=False) for j in range(size)]
    )


def shards(grads, momentum, basis, *, sizes):
    owner = lax.axis_index("replica")
    own = owner.astype(jnp.int32).reshape(1)
    other = 1 - own
    grads = grads[0]
    fsdp, tensor = sizes["fsdp"], sizes["tensor"]
    rank = basis.shape[-1]
    bits = bits_of(fsdp)
    orders = [bits, bits[::-1]]
    product = functools.partial(lax.dot_general, preferred_element_type=jnp.float32)
    switch = functools.partial(swap, axis="replica", bit=1, size=2)

    leaving, mine = partial_projection(own, grads, momentum, basis)
    summed = added(mine, switch(leaving))
    theirs = switch(after(grads, summed))

    def blend(tied):
        pick = functools.partial(lax.dynamic_index_in_dim, index=owner, axis=0, keepdims=False)
        held, got = after((grads, theirs), tied)
        return (
            pick(momentum).astype(jnp.float32) + (pick(held).astype(jnp.float32) + pick(got).astype(jnp.float32))
        ).astype(jnp.bfloat16)

    keep, arrived = scatter_sum(summed, "tensor", tensor)
    piece = sum_of(keep, arrived).astype(jnp.bfloat16)
    arrived = [swap(piece, "tensor", d, tensor) for d in offsets(tensor)]
    blended_own = blend(piece)
    blended_other = switch(blended_own)
    arrived = after(arrived, blended_own)
    projected = gather_rows(piece, arrived, "tensor", tensor)

    place = lax.axis_index("fsdp").astype(jnp.int32)
    ends = [jnp.where(place & order[0], 1, 0) for order in orders]
    held = jnp.stack([ends[0], 2 + ends[1]]).astype(jnp.int32)
    missing = jnp.stack([1 - ends[0], 3 - ends[1]]).astype(jnp.int32)

    gram = product(projected, projected, COLUMNS_BY_COLUMNS).astype(jnp.bfloat16)
    half = rank // 2
    grams = [gram[:half], gram[half:]]
    send = keep = None
    for number in range(len(bits)):
        received = [swap(value, "fsdp", order[number], fsdp) for value, order in zip(grams, orders)]
        if number == 0:
            send = cross(missing, blended_own, after(projected, grams))
            received = after(received, send)
        if number == 1:
            keep = cross(held, blended_own, after(projected, grams, send))
            received = after(received, keep)
        grams = [added(value, got) for value, got in zip(grams, received)]
    work = jnp.concatenate(grams)
    steps = butterfly(orders)
    send = after(send, work)
    received = sent([(None, value) for value in send], "fsdp", fsdp, steps[0])
    todo = list(range(rank // LANES))
    turns = [3] + [1] * len(todo)
    pairs = list(zip(keep, send))

    def shares(squares, axis, size):
        return [swap(squares, axis, d, size) for d in offsets(size)]

    for number, step in enumerate(steps):
        if number > 0:
            pairs = outgoing(values, "fsdp", step)
            received = sent(pairs, "fsdp", fsdp, step)
        for _ in range(min(turns[number] if number < len(turns) else 0, len(todo))):
            work = chol_step(after(work, [pair[1] for pair in pairs]), todo.pop(0), rank)
        received = after(received, work)
        if number == len(bits):
            while todo:
                work = chol_step(work, todo.pop(0), rank)
            high, low = work
            _, squares = times_inverse(*after(values, [pair[1] for pair in pairs]), high, low)
            half = projected.shape[0] // 2
            others = shares(squares, "fsdp", fsdp)
            left, _ = times_inverse(*after((projected[:half], projected[half:]), squares), high, low)
            squares = sum_of(squares, after(others, left))
            received = after(received, (left, squares))
        if number == len(steps) - 1:
            break
        values = incoming(pairs, received, "fsdp", step)

    scale = math.sqrt(grads.shape[1] * fsdp * grads.shape[2] * tensor / rank)
    others = shares(squares, "tensor", tensor)
    back_held, _ = times_inverse(*after(values, (left, squares)), high, low)
    squares = sum_of(squares, after(others, back_held))
    inverse = 1.0 / (jnp.sqrt(squares) + 1e-06)
    outputs = write(own, held, [(left, back_held, blended_own, inverse)], (), scale)

    received = after(received, outputs)
    left_other = switch(after(left, received))
    back_held_other = switch(after(back_held, received))
    inverse_other = switch(after(inverse, received))
    back_got, _ = times_inverse(*received, high, low)
    back_got_other = switch(back_got)
    outputs = write(
        own, missing, [(left, back_got, blended_own, inverse)], outputs, scale
    )
    return tuple(
        write(
            jnp.concatenate([other, other]),
            jnp.concatenate([held, missing]),
            [
                (left_other, back_held_other, blended_other, inverse_other),
                (left_other, back_got_other, blended_other, inverse_other),
            ],
            outputs,
            scale,
        )
    )


def solution(mesh):
    placed = (
        P("replica", None, "fsdp", "tensor"),
        P(None, "fsdp", "tensor"),
        P(None, "tensor", None),
    )
    return jax.shard_map(
        functools.partial(shards, sizes=dict(mesh.shape)),
        mesh=mesh,
        in_specs=placed,
        out_specs=(P(None, "fsdp", "tensor"), P(None, "fsdp", "tensor"), P(None, "tensor", None)),
        check_vma=False,
    )
```

```python
import functools
import math

import jax
import jax.numpy as jnp
from jax import lax
from jax.experimental import pallas as pl
from jax.experimental.pallas import tpu as pltpu
from jax.sharding import PartitionSpec as P

LANES = 128
SUBS = 8
BLOCKS = 4
momentum_decay = 0.95


def invert_block(rows):
    count = len(rows)
    lane = lax.broadcasted_iota(jnp.int32, (SUBS, LANES), 1)
    sub = lax.broadcasted_iota(jnp.int32, (SUBS, LANES), 0)
    rows = list(rows)
    wide = lambda v, i: jnp.broadcast_to(v[i:i+1, :], (SUBS, LANES))
    col = lambda v, c: jnp.broadcast_to(v[:, c:c+1], (SUBS, LANES))
    for p in range(count):
        base = p * SUBS
        inside = (lane >= base) & (lane < base + SUBS)
        mine = rows[p]
        cols = [col(mine, base + i) for i in range(SUBS)]
        solved = jnp.where(inside, jnp.where(lane == base + sub, 1.0, 0.0), mine)
        half = solved
        for i in range(SUBS):
            pivot = wide(cols[i], i)
            inverse = 1.0 / pivot
            at = sub == i
            gain = jnp.where(at, 1.0 - inverse, cols[i] * inverse)
            for j in range(i + 1, SUBS):
                cols[j] = cols[j] - gain * wide(cols[j], i)
            row = wide(solved, i)
            half = jnp.where(at, row * lax.rsqrt(pivot), half)
            solved = solved - gain * row
        rows[p] = jnp.where(lane < base + SUBS, half, 0.0)
        if p + 1 < count:
            wides = [wide(solved, i) for i in range(SUBS)]
            for q in range(p + 1, count):
                below = rows[q]
                terms = [col(below, base + i) * wides[i] for i in range(SUBS)]
                while len(terms) > 1:
                    terms = [a + b for a, b in zip(terms[::2], terms[1::2])]
                rows[q] = jnp.where(inside, 0.0, below) - terms[0]
    return rows


def chol_kernel(*refs, k, blocks):
    last = k == blocks - 1
    source, part = refs[0], refs[-1]
    work = refs[1]
    if k == 0:
        for c in range(blocks):
            work[c] = source[:, c * LANES : (c + 1) * LANES].astype(jnp.float32)
        held = work
    else:
        held = source
    dot = functools.partial(lax.dot_general, preferred_element_type=jnp.float32, precision=lax.Precision.HIGHEST)
    start = k * LANES
    mine = slice(start, start + LANES)
    inv = jnp.concatenate(
        invert_block([held[k, start + SUBS * q : start + SUBS * (q + 1), :] for q in range(LANES // SUBS)]), axis=0
    )
    for c in range(blocks):
        part[c] = inv if c == k else dot(inv, held[c, mine, :], (((1,), (0,)), ((), ())))
    if not last:
        for c in range(blocks):
            if k > 0:
                work[c, :start, :] = held[c, :start, :]
            work[c, mine, :] = part[c]
        for r in range(k + 1, blocks):
            rows = slice(r * LANES, (r + 1) * LANES)
            for c in range(blocks):
                if c > k and c < r:
                    continue
                product = dot(part[r], part[c], (((0,), (0,)), ((), ())))
                work[c, rows, :] = -product if c == k else held[c, rows, :] - product
        return
    high_ref, low_ref = refs[1:3]
    for r in range(blocks):
        rows = slice(r * LANES, (r + 1) * LANES)
        for c in range(blocks):
            cut = slice(c * LANES, (c + 1) * LANES)
            if c > r:
                high_ref[rows, cut] = jnp.zeros((LANES, LANES), jnp.bfloat16)
                low_ref[rows, cut] = jnp.zeros((LANES, LANES), jnp.bfloat16)
                continue
            value = part[c] if r == k else held[c, rows, :]
            high = value.astype(jnp.bfloat16)
            high_ref[rows, cut] = high
            low_ref[rows, cut] = (value - high.astype(jnp.float32)).astype(jnp.bfloat16)


def chol_step(value, k, size):
    blocks = size // LANES
    if k == blocks - 1:
        out_shape = [jax.ShapeDtypeStruct((size, size), jnp.bfloat16)] * 2
    else:
        out_shape = [jax.ShapeDtypeStruct((blocks, size, LANES), jnp.float32)]
    results = pl.pallas_call(
        functools.partial(chol_kernel, k=k, blocks=blocks),
        out_shape=out_shape,
        in_specs=[pl.BlockSpec(memory_space=pltpu.VMEM)],
        out_specs=[pl.BlockSpec(memory_space=pltpu.VMEM)] * len(out_shape),
        scratch_shapes=[pltpu.VMEM((blocks, LANES, LANES), jnp.float32)],
        compiler_params=pltpu.CompilerParams(vmem_limit_bytes=6 << 20),
        name="chol_step",
    )(value)
    return results if k == blocks - 1 else results[0]


def partial_kernel(which_ref, grads_ref, moment_ref, basis_ref, sent_ref, mine_ref):
    @pl.when(pl.program_id(0) == 0)
    def _():
        sent_ref[...] = jnp.dot(grads_ref[...], basis_ref[...], preferred_element_type=jnp.float32).astype(jnp.bfloat16)

    @pl.when(pl.program_id(0) == 1)
    def _():
        rows = (grads_ref[...].astype(jnp.float32) + moment_ref[...].astype(jnp.float32)).astype(jnp.bfloat16)
        mine_ref[...] = jnp.dot(rows, basis_ref[...], preferred_element_type=jnp.float32).astype(jnp.bfloat16)


def partial_projection(own, grads, moment, basis):
    _, rows, units = grads.shape
    rank = basis.shape[-1]
    parts = 2
    tile = rows // parts

    def weight_of(weight, own_ref):
        return jnp.where(weight == 0, 1 - own_ref[0], own_ref[0])

    return pl.pallas_call(
        partial_kernel,
        grid_spec=pltpu.PrefetchScalarGridSpec(
            num_scalar_prefetch=1,
            grid=(2, parts),
            in_specs=[
                pl.BlockSpec((None, tile, units), lambda weight, step, own_ref: (weight_of(weight, own_ref), step, 0)),
                pl.BlockSpec((None, tile, units), lambda weight, step, own_ref: (own_ref[0], step * weight, 0)),
                pl.BlockSpec((None, units, rank), lambda weight, step, own_ref: (weight_of(weight, own_ref), 0, 0)),
            ],
            out_specs=[
                pl.BlockSpec((tile, rank), lambda weight, step, own_ref: (jnp.where(weight == 0, step, parts - 1), 0)),
                pl.BlockSpec((tile, rank), lambda weight, step, own_ref: (step * weight, 0)),
            ],
        ),
        out_shape=[jax.ShapeDtypeStruct((rows, rank), jnp.bfloat16)] * 2,
        compiler_params=pltpu.CompilerParams(vmem_limit_bytes=ROOMY),
        name="partial_projection",
    )(own, grads, moment, basis)


ROWS_BY_ROWS = (((1,), (1,)), ((), ()))
COLUMNS_BY_COLUMNS = (((0,), (0,)), ((), ()))
ROOMY = 48 << 20
SNUG = 24 << 20


def fixed(shape):
    return pl.BlockSpec(shape, lambda step, *_: (0,) * len(shape))


def cross_kernel(ids_ref, blended_ref, projected_ref, first_ref, second_ref):
    product = lax.dot_general(
        blended_ref[...], projected_ref[...], COLUMNS_BY_COLUMNS, preferred_element_type=jnp.float32
    ).astype(jnp.bfloat16)
    for step, ref in enumerate((first_ref, second_ref)):

        @pl.when(pl.program_id(0) == step)
        def _():
            ref[...] = product


def cross(ids, blended, projected):
    rows, rank = projected.shape
    block = blended.shape[1] // BLOCKS
    return pl.pallas_call(
        cross_kernel,
        grid_spec=pltpu.PrefetchScalarGridSpec(
            num_scalar_prefetch=1,
            grid=(2,),
            in_specs=[pl.BlockSpec((rows, block), lambda step, ids_ref: (0, ids_ref[step])), fixed((rows, rank))],
            out_specs=[fixed((block, rank))] * 2,
        ),
        out_shape=[jax.ShapeDtypeStruct((block, rank), jnp.bfloat16)] * 2,
        compiler_params=pltpu.CompilerParams(vmem_limit_bytes=ROOMY),
        name="cross",
    )(ids, blended, projected)


def back_kernel(first_ref, second_ref, high_ref, low_ref, back_ref, squares_ref):
    step = pl.program_id(0)

    def run(ref):
        rows = ref[...]
        back = lax.dot_general(rows, high_ref[...], ROWS_BY_ROWS, preferred_element_type=jnp.float32)
        back += lax.dot_general(rows, low_ref[...], ROWS_BY_ROWS, preferred_element_type=jnp.float32)
        back_ref[...] = back.astype(jnp.bfloat16)
        return jnp.sum(back * back, axis=0, keepdims=True)

    @pl.when(step == 0)
    def _():
        squares_ref[...] = run(first_ref)

    @pl.when(step == 1)
    def _():
        squares_ref[...] += run(second_ref)


def times_inverse(first, second, high, low):
    block, rank = first.shape
    return pl.pallas_call(
        back_kernel,
        grid=(2,),
        in_specs=[fixed((block, rank))] * 2 + [fixed((rank, rank))] * 2,
        out_specs=[pl.BlockSpec((block, rank), lambda step: (step, 0)), fixed((1, rank))],
        out_shape=[jax.ShapeDtypeStruct((2 * block, rank), jnp.bfloat16), jax.ShapeDtypeStruct((1, rank), jnp.float32)],
        compiler_params=pltpu.CompilerParams(vmem_limit_bytes=SNUG),
        name="times_inverse",
    )(first, second, high, low)


def write_kernel(which_ref, ids_ref, *refs, groups, scale):
    momentum_ref, update_ref, basis_ref = refs[-3:]
    for group in range(groups):
        left_ref, back_ref, blended_ref, inverse_ref = refs[4 * group : 4 * (group + 1)]

        @pl.when(pl.program_id(0) // 2 == group)
        def _():
            feedback = lax.dot_general(left_ref[...], back_ref[...], ROWS_BY_ROWS, preferred_element_type=jnp.float32)
            momentum_ref[...] = (
                blended_ref[...].astype(jnp.float32) - (1.0 - momentum_decay) * feedback
            ).astype(jnp.bfloat16)
            normed = (back_ref[...].astype(jnp.float32) * inverse_ref[...]).astype(jnp.bfloat16)
            basis_ref[...] = normed
            product = lax.dot_general(left_ref[...], normed, ROWS_BY_ROWS, preferred_element_type=jnp.float32)
            update_ref[...] = (scale * product).astype(jnp.bfloat16)


def write(which, ids, groups, earlier, scale):
    rows, rank = groups[0][0].shape
    block = groups[0][1].shape[0] // 2
    units = BLOCKS * block
    specs = []
    for group in range(len(groups)):

        def local(step, group=group):
            return jnp.clip(step - 2 * group, 0, 1)

        specs += [
            fixed((rows, rank)),
            pl.BlockSpec((block, rank), lambda step, w, i, local=local: (local(step), 0)),
            pl.BlockSpec((rows, block), lambda step, w, i, local=local, group=group: (0, i[2 * group + local(step)])),
            fixed((1, rank)),
        ]
    columns = pl.BlockSpec((None, rows, block), lambda step, w, i: (w[step // 2], 0, i[step]))
    wide = jax.ShapeDtypeStruct((2, rows, units), jnp.bfloat16)
    out_specs = [columns, columns, pl.BlockSpec((None, block, rank), lambda step, w, i: (w[step // 2], i[step], 0))]
    out_shape = [wide, wide, jax.ShapeDtypeStruct((2, units, rank), jnp.bfloat16)]
    flat = [value for group in groups for value in group]
    return pl.pallas_call(
        functools.partial(write_kernel, groups=len(groups), scale=scale),
        grid_spec=pltpu.PrefetchScalarGridSpec(
            num_scalar_prefetch=2,
            grid=(2 * len(groups),),
            in_specs=specs + [pl.BlockSpec(memory_space=pl.ANY)] * len(earlier),
            out_specs=out_specs,
        ),
        out_shape=out_shape,
        input_output_aliases={2 + len(flat) + i: i for i in range(len(earlier))},
        compiler_params=pltpu.CompilerParams(vmem_limit_bytes=SNUG),
        name="write",
    )(which, ids, *flat, *earlier)


def swap(value, axis, bit, size):
    return lax.ppermute(value, axis, [(i, i ^ bit) for i in range(size)])


def bits_of(size):
    return [1 << i for i in range(size.bit_length() - 1)]


def added(first, second):
    return (first.astype(jnp.float32) + second.astype(jnp.float32)).astype(first.dtype)


def halved(value, axis, bit):
    high = (lax.axis_index(axis) & bit) != 0
    size = value.shape[0] // 2
    first, second = value[:size], value[size:]
    return jnp.where(high, second, first), jnp.where(high, first, second)


def joined(mine, theirs, axis, bit):
    high = (lax.axis_index(axis) & bit) != 0
    return jnp.where(high, jnp.concatenate([theirs, mine]), jnp.concatenate([mine, theirs]))


def after(value, *earlier):
    return lax.optimization_barrier((value, earlier))[0]


def butterfly(orders):
    steps = [(True, [order[i] for order in orders]) for i in range(len(orders[0]))]
    return steps + [(False, bits) for _, bits in reversed(steps)]


def outgoing(values, axis, step):
    reduces, bits = step
    return [halved(value, axis, bit) if reduces else (value, value) for value, bit in zip(values, bits)]


def sent(pairs, axis, size, step):
    return [swap(pair[1], axis, bit, size) for pair, bit in zip(pairs, step[1])]


def incoming(pairs, received, axis, step):
    reduces, bits = step
    return [
        added(pair[0], got) if reduces else joined(pair[0], got, axis, bit)
        for pair, got, bit in zip(pairs, received, bits)
    ]


def offsets(size):
    return sorted(range(1, size), reverse=True)


def scatter_sum(value, axis, size):
    place = lax.axis_index(axis)
    pieces = value.reshape(size, value.shape[0] // size, value.shape[1])
    pick = functools.partial(lax.dynamic_index_in_dim, axis=0, keepdims=False)
    return pick(pieces, place), [swap(pick(pieces, place ^ d), axis, d, size) for d in offsets(size)]


def sum_of(mine, arrived):
    total = mine.astype(jnp.float32)
    for value in arrived:
        total += value.astype(jnp.float32)
    return total


def gather_rows(mine, arrived, axis, size):
    place = lax.axis_index(axis)
    slots = [mine] + [None] * (size - 1)
    for d, value in zip(offsets(size), arrived):
        slots[d] = value
    slots = jnp.stack(slots)
    return jnp.concatenate(
        [lax.dynamic_index_in_dim(slots, place ^ j, axis=0, keepdims=False) for j in range(size)]
    )


def shards(grads, momentum, basis, *, sizes):
    owner = lax.axis_index("replica")
    own = owner.astype(jnp.int32).reshape(1)
    other = 1 - own
    grads = grads[0]
    fsdp, tensor = sizes["fsdp"], sizes["tensor"]
    rank = basis.shape[-1]
    bits = bits_of(fsdp)
    orders = [bits, bits[::-1]]
    product = functools.partial(lax.dot_general, preferred_element_type=jnp.float32)
    switch = functools.partial(swap, axis="replica", bit=1, size=2)

    leaving, mine = partial_projection(own, grads, momentum, basis)
    summed = added(mine, switch(leaving))
    theirs = switch(after(grads, summed))

    def blend(tied):
        pick = functools.partial(lax.dynamic_index_in_dim, index=owner, axis=0, keepdims=False)
        held, got = after((grads, theirs), tied)
        return (
            pick(momentum).astype(jnp.float32) + (pick(held).astype(jnp.float32) + pick(got).astype(jnp.float32))
        ).astype(jnp.bfloat16)

    keep, arrived = scatter_sum(summed, "tensor", tensor)
    piece = sum_of(keep, arrived).astype(jnp.bfloat16)
    arrived = [swap(piece, "tensor", d, tensor) for d in offsets(tensor)]
    blended_own = blend(piece)
    blended_other = switch(blended_own)
    arrived = after(arrived, blended_own)
    projected = gather_rows(piece, arrived, "tensor", tensor)

    place = lax.axis_index("fsdp").astype(jnp.int32)
    ends = [jnp.where(place & order[0], 1, 0) for order in orders]
    held = jnp.stack([ends[0], 2 + ends[1]]).astype(jnp.int32)
    missing = jnp.stack([1 - ends[0], 3 - ends[1]]).astype(jnp.int32)

    gram = product(projected, projected, COLUMNS_BY_COLUMNS).astype(jnp.bfloat16)
    half = rank // 2
    grams = [gram[:half], gram[half:]]
    send = keep = None
    for number in range(len(bits)):
        received = [swap(value, "fsdp", order[number], fsdp) for value, order in zip(grams, orders)]
        if number == 0:
            send = cross(missing, blended_own, after(projected, grams))
            received = after(received, send)
        if number == 1:
            keep = cross(held, blended_own, after(projected, grams, send))
            received = after(received, keep)
        grams = [added(value, got) for value, got in zip(grams, received)]
    work = jnp.concatenate(grams)
    steps = butterfly(orders)
    send = after(send, work)
    received = sent([(None, value) for value in send], "fsdp", fsdp, steps[0])
    todo = list(range(rank // LANES))
    turns = [3] + [1] * len(todo)
    pairs = list(zip(keep, send))

    def shares(squares, axis, size):
        return [swap(squares, axis, d, size) for d in offsets(size)]

    for number, step in enumerate(steps):
        if number > 0:
            pairs = outgoing(values, "fsdp", step)
            received = sent(pairs, "fsdp", fsdp, step)
        for _ in range(min(turns[number] if number < len(turns) else 0, len(todo))):
            work = chol_step(after(work, [pair[1] for pair in pairs]), todo.pop(0), rank)
        received = after(received, work)
        if number == len(bits):
            while todo:
                work = chol_step(work, todo.pop(0), rank)
            high, low = work
            _, squares = times_inverse(*after(values, [pair[1] for pair in pairs]), high, low)
            half = projected.shape[0] // 2
            others = shares(squares, "fsdp", fsdp)
            left, _ = times_inverse(*after((projected[:half], projected[half:]), squares), high, low)
            squares = sum_of(squares, after(others, left))
            received = after(received, (left, squares))
        if number == len(steps) - 1:
            break
        values = incoming(pairs, received, "fsdp", step)

    scale = math.sqrt(grads.shape[1] * fsdp * grads.shape[2] * tensor / rank)
    others = shares(squares, "tensor", tensor)
    back_held, _ = times_inverse(*after(values, (left, squares)), high, low)
    squares = sum_of(squares, after(others, back_held))
    inverse = 1.0 / (jnp.sqrt(squares) + 1e-06)
    outputs = write(own, held, [(left, back_held, blended_own, inverse)], (), scale)

    received = after(received, outputs)
    left_other = switch(after(left, received))
    back_held_other = switch(after(back_held, received))
    inverse_other = switch(after(inverse, received))
    back_got, _ = times_inverse(*received, high, low)
    back_got_other = switch(back_got)
    outputs = write(
        own, missing, [(left, back_got, blended_own, inverse)], outputs, scale
    )
    return tuple(
        write(
            jnp.concatenate([other, other]),
            jnp.concatenate([held, missing]),
            [
                (left_other, back_held_other, blended_other, inverse_other),
                (left_other, back_got_other, blended_other, inverse_other),
            ],
            outputs,
            scale,
        )
    )


def solution(mesh):
    placed = (
        P("replica", None, "fsdp", "tensor"),
        P(None, "fsdp", "tensor"),
        P(None, "tensor", None),
    )
    return jax.shard_map(
        functools.partial(shards, sizes=dict(mesh.shape)),
        mesh=mesh,
        in_specs=placed,
        out_specs=(P(None, "fsdp", "tensor"), P(None, "fsdp", "tensor"), P(None, "tensor", None)),
        check_vma=False,
    )
```

```python
import functools
import math

import jax
import jax.numpy as jnp
from jax import lax
from jax.experimental import pallas as pl
from jax.experimental.pallas import tpu as pltpu
from jax.sharding import PartitionSpec as P

LANES = 128
SUBS = 8
BLOCKS = 4
momentum_decay = 0.95


def invert_block(rows):
    count = len(rows)
    lane = lax.broadcasted_iota(jnp.int32, (SUBS, LANES), 1)
    sub = lax.broadcasted_iota(jnp.int32, (SUBS, LANES), 0)
    rows = list(rows)
    wide = lambda v, i: jnp.broadcast_to(v[i:i+1, :], (SUBS, LANES))
    col = lambda v, c: jnp.broadcast_to(v[:, c:c+1], (SUBS, LANES))
    for p in range(count):
        base = p * SUBS
        inside = (lane >= base) & (lane < base + SUBS)
        mine = rows[p]
        cols = [col(mine, base + i) for i in range(SUBS)]
        solved = jnp.where(inside, jnp.where(lane == base + sub, 1.0, 0.0), mine)
        half = solved
        for i in range(SUBS):
            pivot = wide(cols[i], i)
            inverse = 1.0 / pivot
            at = sub == i
            gain = jnp.where(at, 1.0 - inverse, cols[i] * inverse)
            for j in range(i + 1, SUBS):
                cols[j] = cols[j] - gain * wide(cols[j], i)
            row = wide(solved, i)
            half = jnp.where(at, row * lax.rsqrt(pivot), half)
            solved = solved - gain * row
        rows[p] = jnp.where(lane < base + SUBS, half, 0.0)
        if p + 1 < count:
            wides = [wide(solved, i) for i in range(SUBS)]
            for q in range(p + 1, count):
                below = rows[q]
                terms = [col(below, base + i) * wides[i] for i in range(SUBS)]
                while len(terms) > 1:
                    terms = [a + b for a, b in zip(terms[::2], terms[1::2])]
                rows[q] = jnp.where(inside, 0.0, below) - terms[0]
    return rows


def chol_kernel(*refs, k, blocks):
    last = k == blocks - 1
    source, part = refs[0], refs[-1]
    work = refs[1]
    if k == 0:
        for c in range(blocks):
            work[c] = source[:, c * LANES : (c + 1) * LANES].astype(jnp.float32)
        held = work
    else:
        held = source
    dot = functools.partial(lax.dot_general, preferred_element_type=jnp.float32, precision=lax.Precision.HIGHEST)
    start = k * LANES
    mine = slice(start, start + LANES)
    inv = jnp.concatenate(
        invert_block([held[k, start + SUBS * q : start + SUBS * (q + 1), :] for q in range(LANES // SUBS)]), axis=0
    )
    for c in range(blocks):
        part[c] = inv if c == k else dot(inv, held[c, mine, :], (((1,), (0,)), ((), ())))
    if not last:
        for c in range(blocks):
            if k > 0:
                work[c, :start, :] = held[c, :start, :]
            work[c, mine, :] = part[c]
        for r in range(k + 1, blocks):
            rows = slice(r * LANES, (r + 1) * LANES)
            for c in range(blocks):
                if c > k and c < r:
                    continue
                product = dot(part[r], part[c], (((0,), (0,)), ((), ())))
                work[c, rows, :] = -product if c == k else held[c, rows, :] - product
        return
    high_ref, low_ref = refs[1:3]
    for r in range(blocks):
        rows = slice(r * LANES, (r + 1) * LANES)
        for c in range(blocks):
            cut = slice(c * LANES, (c + 1) * LANES)
            if c > r:
                high_ref[rows, cut] = jnp.zeros((LANES, LANES), jnp.bfloat16)
                low_ref[rows, cut] = jnp.zeros((LANES, LANES), jnp.bfloat16)
                continue
            value = part[c] if r == k else held[c, rows, :]
            high = value.astype(jnp.bfloat16)
            high_ref[rows, cut] = high
            low_ref[rows, cut] = (value - high.astype(jnp.float32)).astype(jnp.bfloat16)


def chol_step(value, k, size):
    blocks = size // LANES
    if k == blocks - 1:
        out_shape = [jax.ShapeDtypeStruct((size, size), jnp.bfloat16)] * 2
    else:
        out_shape = [jax.ShapeDtypeStruct((blocks, size, LANES), jnp.float32)]
    results = pl.pallas_call(
        functools.partial(chol_kernel, k=k, blocks=blocks),
        out_shape=out_shape,
        in_specs=[pl.BlockSpec(memory_space=pltpu.VMEM)],
        out_specs=[pl.BlockSpec(memory_space=pltpu.VMEM)] * len(out_shape),
        scratch_shapes=[pltpu.VMEM((blocks, LANES, LANES), jnp.float32)],
        compiler_params=pltpu.CompilerParams(vmem_limit_bytes=6 << 20),
        name="chol_step",
    )(value)
    return results if k == blocks - 1 else results[0]


def partial_kernel(which_ref, grads_ref, moment_ref, basis_ref, sent_ref, mine_ref):
    @pl.when(pl.program_id(0) == 0)
    def _():
        sent_ref[...] = jnp.dot(grads_ref[...], basis_ref[...], preferred_element_type=jnp.float32).astype(jnp.bfloat16)

    @pl.when(pl.program_id(0) == 1)
    def _():
        rows = (grads_ref[...].astype(jnp.float32) + moment_ref[...].astype(jnp.float32)).astype(jnp.bfloat16)
        mine_ref[...] = jnp.dot(rows, basis_ref[...], preferred_element_type=jnp.float32).astype(jnp.bfloat16)


def partial_projection(own, grads, moment, basis):
    _, rows, units = grads.shape
    rank = basis.shape[-1]
    parts = 2
    tile = rows // parts

    def weight_of(weight, own_ref):
        return jnp.where(weight == 0, 1 - own_ref[0], own_ref[0])

    return pl.pallas_call(
        partial_kernel,
        grid_spec=pltpu.PrefetchScalarGridSpec(
            num_scalar_prefetch=1,
            grid=(2, parts),
            in_specs=[
                pl.BlockSpec((None, tile, units), lambda weight, step, own_ref: (weight_of(weight, own_ref), step, 0)),
                pl.BlockSpec((None, tile, units), lambda weight, step, own_ref: (own_ref[0], step * weight, 0)),
                pl.BlockSpec((None, units, rank), lambda weight, step, own_ref: (weight_of(weight, own_ref), 0, 0)),
            ],
            out_specs=[
                pl.BlockSpec((tile, rank), lambda weight, step, own_ref: (jnp.where(weight == 0, step, parts - 1), 0)),
                pl.BlockSpec((tile, rank), lambda weight, step, own_ref: (step * weight, 0)),
            ],
        ),
        out_shape=[jax.ShapeDtypeStruct((rows, rank), jnp.bfloat16)] * 2,
        compiler_params=pltpu.CompilerParams(vmem_limit_bytes=ROOMY),
        name="partial_projection",
    )(own, grads, moment, basis)


ROWS_BY_ROWS = (((1,), (1,)), ((), ()))
COLUMNS_BY_COLUMNS = (((0,), (0,)), ((), ()))
ROOMY = 48 << 20
SNUG = 24 << 20


def fixed(shape):
    return pl.BlockSpec(shape, lambda step, *_: (0,) * len(shape))


def cross_kernel(ids_ref, blended_ref, projected_ref, first_ref, second_ref):
    product = lax.dot_general(
        blended_ref[...], projected_ref[...], COLUMNS_BY_COLUMNS, preferred_element_type=jnp.float32
    ).astype(jnp.bfloat16)
    for step, ref in enumerate((first_ref, second_ref)):

        @pl.when(pl.program_id(0) == step)
        def _():
            ref[...] = product


def cross(ids, blended, projected):
    rows, rank = projected.shape
    block = blended.shape[1] // BLOCKS
    return pl.pallas_call(
        cross_kernel,
        grid_spec=pltpu.PrefetchScalarGridSpec(
            num_scalar_prefetch=1,
            grid=(2,),
            in_specs=[pl.BlockSpec((rows, block), lambda step, ids_ref: (0, ids_ref[step])), fixed((rows, rank))],
            out_specs=[fixed((block, rank))] * 2,
        ),
        out_shape=[jax.ShapeDtypeStruct((block, rank), jnp.bfloat16)] * 2,
        compiler_params=pltpu.CompilerParams(vmem_limit_bytes=ROOMY),
        name="cross",
    )(ids, blended, projected)


def back_kernel(first_ref, second_ref, high_ref, low_ref, back_ref, squares_ref):
    step = pl.program_id(0)

    def run(ref):
        rows = ref[...]
        back = lax.dot_general(rows, high_ref[...], ROWS_BY_ROWS, preferred_element_type=jnp.float32)
        back += lax.dot_general(rows, low_ref[...], ROWS_BY_ROWS, preferred_element_type=jnp.float32)
        back_ref[...] = back.astype(jnp.bfloat16)
        return jnp.sum(back * back, axis=0, keepdims=True)

    @pl.when(step == 0)
    def _():
        squares_ref[...] = run(first_ref)

    @pl.when(step == 1)
    def _():
        squares_ref[...] += run(second_ref)


def times_inverse(first, second, high, low):
    block, rank = first.shape
    return pl.pallas_call(
        back_kernel,
        grid=(2,),
        in_specs=[fixed((block, rank))] * 2 + [fixed((rank, rank))] * 2,
        out_specs=[pl.BlockSpec((block, rank), lambda step: (step, 0)), fixed((1, rank))],
        out_shape=[jax.ShapeDtypeStruct((2 * block, rank), jnp.bfloat16), jax.ShapeDtypeStruct((1, rank), jnp.float32)],
        compiler_params=pltpu.CompilerParams(vmem_limit_bytes=SNUG),
        name="times_inverse",
    )(first, second, high, low)


def write_kernel(which_ref, ids_ref, *refs, groups, scale):
    momentum_ref, update_ref, basis_ref = refs[-3:]
    for group in range(groups):
        left_ref, back_ref, blended_ref, inverse_ref = refs[4 * group : 4 * (group + 1)]

        @pl.when(pl.program_id(0) // 2 == group)
        def _():
            feedback = lax.dot_general(left_ref[...], back_ref[...], ROWS_BY_ROWS, preferred_element_type=jnp.float32)
            momentum_ref[...] = (
                blended_ref[...].astype(jnp.float32) - (1.0 - momentum_decay) * feedback
            ).astype(jnp.bfloat16)
            normed = (back_ref[...].astype(jnp.float32) * inverse_ref[...]).astype(jnp.bfloat16)
            basis_ref[...] = normed
            product = lax.dot_general(left_ref[...], normed, ROWS_BY_ROWS, preferred_element_type=jnp.float32)
            update_ref[...] = (scale * product).astype(jnp.bfloat16)


def write(which, ids, groups, earlier, scale):
    rows, rank = groups[0][0].shape
    block = groups[0][1].shape[0] // 2
    units = BLOCKS * block
    specs = []
    for group in range(len(groups)):

        def local(step, group=group):
            return jnp.clip(step - 2 * group, 0, 1)

        specs += [
            fixed((rows, rank)),
            pl.BlockSpec((block, rank), lambda step, w, i, local=local: (local(step), 0)),
            pl.BlockSpec((rows, block), lambda step, w, i, local=local, group=group: (0, i[2 * group + local(step)])),
            fixed((1, rank)),
        ]
    columns = pl.BlockSpec((None, rows, block), lambda step, w, i: (w[step // 2], 0, i[step]))
    wide = jax.ShapeDtypeStruct((2, rows, units), jnp.bfloat16)
    out_specs = [columns, columns, pl.BlockSpec((None, block, rank), lambda step, w, i: (w[step // 2], i[step], 0))]
    out_shape = [wide, wide, jax.ShapeDtypeStruct((2, units, rank), jnp.bfloat16)]
    flat = [value for group in groups for value in group]
    return pl.pallas_call(
        functools.partial(write_kernel, groups=len(groups), scale=scale),
        grid_spec=pltpu.PrefetchScalarGridSpec(
            num_scalar_prefetch=2,
            grid=(2 * len(groups),),
            in_specs=specs + [pl.BlockSpec(memory_space=pl.ANY)] * len(earlier),
            out_specs=out_specs,
        ),
        out_shape=out_shape,
        input_output_aliases={2 + len(flat) + i: i for i in range(len(earlier))},
        compiler_params=pltpu.CompilerParams(vmem_limit_bytes=SNUG),
        name="write",
    )(which, ids, *flat, *earlier)


def swap(value, axis, bit, size):
    return lax.ppermute(value, axis, [(i, i ^ bit) for i in range(size)])


def bits_of(size):
    return [1 << i for i in range(size.bit_length() - 1)]


def added(first, second):
    return (first.astype(jnp.float32) + second.astype(jnp.float32)).astype(first.dtype)


def halved(value, axis, bit):
    high = (lax.axis_index(axis) & bit) != 0
    size = value.shape[0] // 2
    first, second = value[:size], value[size:]
    return jnp.where(high, second, first), jnp.where(high, first, second)


def joined(mine, theirs, axis, bit):
    high = (lax.axis_index(axis) & bit) != 0
    return jnp.where(high, jnp.concatenate([theirs, mine]), jnp.concatenate([mine, theirs]))


def after(value, *earlier):
    return lax.optimization_barrier((value, earlier))[0]


def butterfly(orders):
    steps = [(True, [order[i] for order in orders]) for i in range(len(orders[0]))]
    return steps + [(False, bits) for _, bits in reversed(steps)]


def outgoing(values, axis, step):
    reduces, bits = step
    return [halved(value, axis, bit) if reduces else (value, value) for value, bit in zip(values, bits)]


def sent(pairs, axis, size, step):
    return [swap(pair[1], axis, bit, size) for pair, bit in zip(pairs, step[1])]


def incoming(pairs, received, axis, step):
    reduces, bits = step
    return [
        added(pair[0], got) if reduces else joined(pair[0], got, axis, bit)
        for pair, got, bit in zip(pairs, received, bits)
    ]


def offsets(size):
    return sorted(range(1, size), reverse=True)


def scatter_sum(value, axis, size):
    place = lax.axis_index(axis)
    pieces = value.reshape(size, value.shape[0] // size, value.shape[1])
    pick = functools.partial(lax.dynamic_index_in_dim, axis=0, keepdims=False)
    return pick(pieces, place), [swap(pick(pieces, place ^ d), axis, d, size) for d in offsets(size)]


def sum_of(mine, arrived):
    total = mine.astype(jnp.float32)
    for value in arrived:
        total += value.astype(jnp.float32)
    return total


def gather_rows(mine, arrived, axis, size):
    place = lax.axis_index(axis)
    slots = [mine] + [None] * (size - 1)
    for d, value in zip(offsets(size), arrived):
        slots[d] = value
    slots = jnp.stack(slots)
    return jnp.concatenate(
        [lax.dynamic_index_in_dim(slots, place ^ j, axis=0, keepdims=False) for j in range(size)]
    )


def shards(grads, momentum, basis, *, sizes):
    owner = lax.axis_index("replica")
    own = owner.astype(jnp.int32).reshape(1)
    other = 1 - own
    grads = grads[0]
    fsdp, tensor = sizes["fsdp"], sizes["tensor"]
    rank = basis.shape[-1]
    bits = bits_of(fsdp)
    orders = [bits, bits[::-1]]
    product = functools.partial(lax.dot_general, preferred_element_type=jnp.float32)
    switch = functools.partial(swap, axis="replica", bit=1, size=2)

    leaving, mine = partial_projection(own, grads, momentum, basis)
    summed = added(mine, switch(leaving))
    theirs = switch(after(grads, summed))

    def blend(tied):
        pick = functools.partial(lax.dynamic_index_in_dim, index=owner, axis=0, keepdims=False)
        held, got = after((grads, theirs), tied)
        return (
            pick(momentum).astype(jnp.float32) + (pick(held).astype(jnp.float32) + pick(got).astype(jnp.float32))
        ).astype(jnp.bfloat16)

    keep, arrived = scatter_sum(summed, "tensor", tensor)
    piece = sum_of(keep, arrived).astype(jnp.bfloat16)
    arrived = [swap(piece, "tensor", d, tensor) for d in offsets(tensor)]
    blended_own = blend(piece)
    blended_other = switch(blended_own)
    arrived = after(arrived, blended_own)
    projected = gather_rows(piece, arrived, "tensor", tensor)

    place = lax.axis_index("fsdp").astype(jnp.int32)
    ends = [jnp.where(place & order[0], 1, 0) for order in orders]
    held = jnp.stack([ends[0], 2 + ends[1]]).astype(jnp.int32)
    missing = jnp.stack([1 - ends[0], 3 - ends[1]]).astype(jnp.int32)

    gram = product(projected, projected, COLUMNS_BY_COLUMNS).astype(jnp.bfloat16)
    half = rank // 2
    grams = [gram[:half], gram[half:]]
    send = keep = None
    for number in range(len(bits)):
        received = [swap(value, "fsdp", order[number], fsdp) for value, order in zip(grams, orders)]
        if number == 0:
            send = cross(missing, blended_own, after(projected, grams))
            received = after(received, send)
        if number == 1:
            keep = cross(held, blended_own, after(projected, grams, send))
            received = after(received, keep)
        grams = [added(value, got) for value, got in zip(grams, received)]
    work = jnp.concatenate(grams)
    steps = butterfly(orders)
    send = after(send, work)
    received = sent([(None, value) for value in send], "fsdp", fsdp, steps[0])
    todo = list(range(rank // LANES))
    turns = [3] + [1] * len(todo)
    pairs = list(zip(keep, send))

    for number, step in enumerate(steps):
        if number > 0:
            pairs = outgoing(values, "fsdp", step)
            received = sent(pairs, "fsdp", fsdp, step)
        for _ in range(min(turns[number] if number < len(turns) else 0, len(todo))):
            work = chol_step(after(work, [pair[1] for pair in pairs]), todo.pop(0), rank)
        received = after(received, work)
        if number == len(bits):
            while todo:
                work = chol_step(work, todo.pop(0), rank)
            high, low = work
            _, squares = times_inverse(*after(values, [pair[1] for pair in pairs]), high, low)
            half = projected.shape[0] // 2
            for bit in bits:
                squares = squares + swap(squares, "fsdp", bit, fsdp)
            received = after(received, squares)
        if number == len(steps) - 1:
            break
        values = incoming(pairs, received, "fsdp", step)

    scale = math.sqrt(grads.shape[1] * fsdp * grads.shape[2] * tensor / rank)
    half = projected.shape[0] // 2
    left, _ = times_inverse(*after((projected[:half], projected[half:]), (values, squares)), high, low)
    for bit in bits_of(tensor)[:-1]:
        squares = squares + after(swap(squares, "tensor", bit, tensor), left)
    back_held, _ = times_inverse(*after(values, (left, squares)), high, low)
    for bit in bits_of(tensor)[-1:]:
        squares = squares + after(swap(squares, "tensor", bit, tensor), back_held)
    inverse = 1.0 / (jnp.sqrt(squares) + 1e-06)
    outputs = write(own, held, [(left, back_held, blended_own, inverse)], (), scale)

    received = after(received, outputs)
    left_other = switch(after(left, received))
    back_held_other = switch(after(back_held, received))
    inverse_other = switch(after(inverse, received))
    back_got, _ = times_inverse(*received, high, low)
    back_got_other = switch(back_got)
    outputs = write(
        own, missing, [(left, back_got, blended_own, inverse)], outputs, scale
    )
    return tuple(
        write(
            jnp.concatenate([other, other]),
            jnp.concatenate([held, missing]),
            [
                (left_other, back_held_other, blended_other, inverse_other),
                (left_other, back_got_other, blended_other, inverse_other),
            ],
            outputs,
            scale,
        )
    )


def solution(mesh):
    placed = (
        P("replica", None, "fsdp", "tensor"),
        P(None, "fsdp", "tensor"),
        P(None, "tensor", None),
    )
    return jax.shard_map(
        functools.partial(shards, sizes=dict(mesh.shape)),
        mesh=mesh,
        in_specs=placed,
        out_specs=(P(None, "fsdp", "tensor"), P(None, "fsdp", "tensor"), P(None, "tensor", None)),
        check_vma=False,
    )
```
